128 devices in a mesh: pool: 4 (over x), section: 4 (over y_hi, core), tp: 8 (over z, y_lo).
Axes of the slice: x: 4, y: 4 (y_hi: 2, y_lo: 2; y = y_hi * 2 + y_lo), z: 4, core: 2. Of those that a mesh axis runs over, the one named last changes fastest.
Arguments:
- frames: bfloat16 [4, 4, 256, 1280], P('pool', 'section'), may hold values from -6 to 6
- ln_gain: bfloat16 [1280], replicated, may hold values from 0.25 to 1.75
- ln_bias: bfloat16 [1280], replicated, may hold values from -4 to 4
- enc_up: bfloat16 [1280, 5120], P(None, 'tp'), may hold values from -0.15625 to 0.15625
- up_bias: bfloat16 [5120], P('tp'), may hold values from -4 to 4
- enc_down: bfloat16 [5120, 1280], P('tp'), may hold values from -0.15625 to 0.15625
- down_bias: bfloat16 [1280], replicated, may hold values from -4 to 4
- adapt_in: bfloat16 [5120, 5120], P(None, ('section', 'tp')), may hold values from -0.078125 to 0.078125
- adapt_out: bfloat16 [5120, 5120], P(('section', 'tp')), may hold values from -0.078125 to 0.078125
- lengths: int32 [4, 4, 8], replicated, may hold values from 1 to 16, 64 in all within a row
- routes: int32 [4, 4, 8, 1], replicated, may hold values from 0 to 3; in each aligned block of 8 rows (0 to 7, 8 to 15, ..., all dimensions but the last counted through in order) at most 2 rows name the same one
- attn_gain: bfloat16 [4, 5120], P('section'), may hold values from 0.25 to 1.75
- q_weight: bfloat16 [4, 5120, 4096], P('section', None, 'tp'), may hold values from -1 to 1
- k_weight: bfloat16 [4, 5120, 1024], P('section', None, 'tp'), may hold values from -4 to 4
- v_weight: bfloat16 [4, 5120, 1024], P('section', None, 'tp'), may hold values from -0.078125 to 0.078125
- o_weight: bfloat16 [4, 4096, 5120], P('section', 'tp'), may hold values from -0.09375 to 0.09375
Outputs:
- decoded: float32 [4, 4, 128, 5120], P('pool', 'section', 'tp')
The draws below stay inside these ranges and needn't reach their ends.
Inputs may be any that keep to these rules, and one draw needn't show every extreme that they name: Each encoder group's lengths sum to 64; the longest window of every group has exactly 16 tokens. `routes`: each encoder group's 8 windows name every prefill group exactly 2 times.
All inputs are finite; a program needn't handle non-finite values.
Results may differ from the reference program's by a relative error of at most 0.034.
Values may be sent and summed in bfloat16 or wider, within the bound.
No kernel may reach another device: no remote copies, remote signals or barrier semaphores. Data moves between devices by JAX's collectives and lax.ppermute only.
A program may use at most 128 MiB of HBM per device.

```python
import math
import jax
import jax.numpy as jnp
import numpy as np
from jax import lax

E = 1280
EF = 5120
D = 5120
HQ = 32
HK = 8
HD = 128
WIN_MAX = 16
WIN = 8
CAPW = 2
LAYERS = 4
GR = 64
FRAMES = 256
D_A = 5120
QD = 4096
KD = 1024
SEQ = 128
N_POOL = 4
N_SECTION = 4
N_TP = 8


def shared_query(key):
    return jax.random.normal(key, (LAYERS, D, HQ * HD), jnp.float32)


def draw_q_weight(key, part):
    common = shared_query(key)
    return (common * D ** (-0.5)).astype(jnp.bfloat16)


def draw_k_weight(key, part):
    key = jax.random.fold_in(key, 12)
    own = jax.random.normal(key, (LAYERS, D, HK * HD), jnp.float32)
    return jnp.clip(own * D ** (-0.5), -4.0, 4.0).astype(jnp.bfloat16)


def level_of(rng, dims, split, low, high):
    def one(axis_at, blocks):
        draws = jax.random.uniform(jax.random.fold_in(jax.random.fold_in(rng, 6), axis_at), (blocks,), jnp.float32, low / len(split), high / len(split))
        return jnp.repeat(jnp.exp(draws), dims[axis_at] // blocks).reshape((-1,) + (1,) * (len(dims) - axis_at - 1))

    gain = one(*split[0])
    for cut in split[1:]:
        gain = gain * one(*cut)
    return gain


def split_up(number_of, total, most, slope):
    weights = [(1 << 20) // math.isqrt(rank ** slope) + 1 for rank in range(2, number_of + 1)]
    surplus, holding = total - most - (number_of - 1), [1] * (number_of - 1)
    while surplus > 0:
        free = [i for i in range(number_of - 1) if holding[i] < most]
        mass, budget = sum([weights[i] for i in free]), surplus
        for i in free:
            addition = min(most - holding[i], max(1, budget * weights[i] // mass), surplus)
            holding[i] = holding[i] + addition
            surplus = surplus - addition
    return np.array([most] + holding)


def uneven_parts(own_key, number_of, total, reach, lean):
    if number_of == 2:
        one = jax.random.randint(own_key, (), max(1, total - reach), min(reach, total - 1) + 1)
        return jnp.stack([one, total - one])
    tallies = jnp.asarray(split_up(number_of, total, reach, lean), jnp.int32)
    pairs = (number_of - 1) // 2
    giver, sink = tallies[1:1 + 2 * pairs:2], tallies[2:2 + 2 * pairs:2]
    slack = jnp.minimum(giver - 1, reach - sink)
    passed = jax.random.randint(jax.random.fold_in(own_key, 1), (pairs,), 0, 1 << 20) % (slack + 1)
    tallies = tallies.at[1:1 + 2 * pairs:2].set(giver - passed).at[2:2 + 2 * pairs:2].set(sink + passed)
    return tallies[jax.random.permutation(jax.random.fold_in(own_key, 2), number_of)]


def deal_out(rng, own, number, rows, number_of, top, most, slope):
    order = jax.random.permutation(rng, number_of)
    heavy_load, usual = load_shares(number_of, rows * top, most, slope, True), load_shares(number_of, rows * top, most, slope, False)
    places = jnp.arange(number_of)

    def named(tallies, turn):
        used = int((tallies > 0).sum())
        fixed = max(1, used // 4)
        shifted = fixed + (places - fixed + turn * (used - fixed)) % max(1, number_of - fixed)
        return jnp.zeros((number_of,), jnp.int32).at[order[jnp.where(places < fixed, places, shifted)]].set(jnp.asarray(tallies, jnp.int32))

    tallies = jnp.where(number % 4 == 0, named(heavy_load, number // 4), named(usual, number - number // 4 - 1))
    mixed = jax.random.permutation(jax.random.fold_in(own, 3), number_of)
    source_of, sink = mixed[0:number_of // 2 * 2:2], mixed[1:number_of // 2 * 2:2]
    margin = jnp.minimum(tallies[source_of] - 1, most - tallies[sink]) // 2
    margin = jnp.where((source_of == order[0]) | (sink == order[0]) | (tallies[sink] == 0), 0, jnp.maximum(margin, 0))
    shifted = jax.random.randint(jax.random.fold_in(own, 4), (number_of // 2,), 0, 1 << 20) % (margin + 1)
    tallies = tallies.at[source_of].add(-shifted).at[sink].add(shifted)
    items = jnp.searchsorted(jnp.cumsum(tallies), jnp.arange(rows * top), side="right").astype(jnp.int32)
    grid = items.reshape(top, rows).T
    grid = grid[jax.random.permutation(jax.random.fold_in(own, 1), rows)]
    turn = jax.random.randint(jax.random.fold_in(own, 2), (rows, 1), 0, top)
    return jnp.take_along_axis(grid, (jnp.arange(top)[None, :] + turn) % top, axis=1)


def load_shares(amount, total, most, skew, full):
    portions = [(1 << 20) // math.isqrt(standing ** skew) + 1 for standing in range(1, amount + 1)]
    largest = most if full else min(most, max(-(-total // amount), total * portions[0] // sum(portions)))
    least = 1 if total - largest >= amount - 1 else 0
    given, spare = [largest] + [least] * (amount - 1), total - largest - least * (amount - 1)
    while spare > 0:
        free = [i for i in range(1, amount) if given[i] < largest] or [i for i in range(1, amount) if given[i] < most]
        mass, budget = sum([portions[i] for i in free]), spare
        for i in free:
            addition = min(most - given[i], max(1, budget * portions[i] // mass), spare)
            given[i] = given[i] + addition
            spare = spare - addition
    return np.array(given)


def bell_draw(stream_key, dims, scale, most, cuts=(), held_as=jnp.bfloat16):
    factor_of = level_of(stream_key, dims, cuts, -0.22, 0.18) if cuts else 1.0
    values = jax.random.normal(stream_key, dims, jnp.float32) * scale * factor_of
    return jnp.minimum(jnp.maximum(values, -most), most).astype(held_as)


def setup_inputs(seed: int = 0) -> dict:
    keys = jax.random.split(jax.random.key(seed), 17)
    frames = bell_draw(keys[0], (N_POOL, LAYERS, FRAMES, E), 1.0, 6.0, ((0, 4), (1, 4)))
    ln_gain = jnp.clip(1.0 + 0.15 * jax.random.normal(keys[1], (E,), jnp.float32), 0.25, 1.75).astype(jnp.bfloat16)
    ln_bias = bell_draw(keys[2], (E,), 0.4, 4.0)
    enc_up = bell_draw(keys[3], (E, EF), E ** -0.5, 0.15625, ((1, 8),))
    up_bias = bell_draw(keys[4], (EF,), 0.5, 4.0, ((0, 8),))
    enc_down = bell_draw(keys[5], (EF, E), (EF // 4) ** -0.5, 0.15625, ((0, 8),))
    down_bias = bell_draw(keys[6], (E,), 0.5, 4.0)
    adapt_in = bell_draw(keys[7], (D_A, D), D_A ** -0.5, 0.078125, ((1, 32),))
    adapt_out = bell_draw(keys[8], (D, D), D ** -0.5, 0.078125, ((0, 32),))
    lengths = jax.vmap(lambda own: uneven_parts(own, WIN, GR, WIN_MAX, 2))(jax.random.split(keys[9], N_POOL * LAYERS)).reshape((N_POOL, LAYERS, WIN)).astype(jnp.int32)
    routes_keys = jax.random.split(jax.random.fold_in(keys[10], 1), N_POOL * LAYERS * WIN // WIN)
    routes_turns = jax.random.permutation(jax.random.fold_in(keys[10], 3), N_POOL * LAYERS * WIN // WIN)
    routes = jax.vmap(lambda own, number: deal_out(jax.random.fold_in(keys[10], 2), own, number, WIN, N_POOL, 1, CAPW, 0))(routes_keys, routes_turns).reshape((N_POOL, LAYERS, WIN, 1))
    attn_gain = jnp.clip(1.0 + 0.15 * jax.random.normal(keys[11], (LAYERS, D), jnp.float32), 0.25, 1.75).astype(jnp.bfloat16)
    q_weight = draw_q_weight(jax.random.fold_in(keys[16], 71), 0)
    k_weight = draw_k_weight(jax.random.fold_in(keys[16], 71), 0)
    v_weight = bell_draw(keys[14], (LAYERS, D, KD), D ** -0.5, 0.078125, ((0, 4), (2, 8)))
    o_weight = bell_draw(keys[15], (LAYERS, QD, D), QD ** -0.5, 0.09375, ((0, 4), (1, 8)))
    return dict(frames=frames, ln_gain=ln_gain, ln_bias=ln_bias, enc_up=enc_up, up_bias=up_bias, enc_down=enc_down, down_bias=down_bias, adapt_in=adapt_in, adapt_out=adapt_out, lengths=lengths, routes=routes, attn_gain=attn_gain, q_weight=q_weight, k_weight=k_weight, v_weight=v_weight, o_weight=o_weight)


EPSILON = 1e-05

def layer_norm(values, gain_row, shift_row):
    mean_value = lax.optimization_barrier(jnp.mean(values, axis=-1, keepdims=True))
    centered = values - mean_value
    variance = lax.optimization_barrier(jnp.mean(centered * centered, axis=-1, keepdims=True))
    return centered * lax.rsqrt(variance + EPSILON) * gain_row + shift_row

def rms_norm(values, gain_row):
    return values * lax.rsqrt(lax.optimization_barrier(jnp.mean(values * values, axis=-1, keepdims=True)) + EPSILON) * gain_row

def slot_tables(route_row, length_row, dest_count, capacity):
    windows = route_row.shape[0]
    window_ids = jnp.arange(windows, dtype=jnp.int32)
    starts = jnp.cumsum(length_row, dtype=jnp.int32) - length_row
    earlier = (route_row[None, :] == route_row[:, None]) & (window_ids[None, :] < window_ids[:, None])
    window_rank = lax.optimization_barrier(jnp.sum(earlier.astype(jnp.int32), axis=1, dtype=jnp.int32))
    dest_ids = jnp.arange(dest_count, dtype=jnp.int32)
    rank_ids = jnp.arange(capacity, dtype=jnp.int32)
    chosen = (route_row[None, None, :] == dest_ids[:, None, None]) & (window_rank[None, None, :] == rank_ids[None, :, None])
    chosen = chosen.astype(jnp.int32)
    return (lax.optimization_barrier(jnp.sum(chosen * starts, axis=2, dtype=jnp.int32)), lax.optimization_barrier(jnp.sum(chosen * length_row, axis=2, dtype=jnp.int32)))

def reference(frames, ln_gain, ln_bias, enc_up, up_bias, enc_down, down_bias, adapt_in, adapt_out, lengths, routes, attn_gain, q_weight, k_weight, v_weight, o_weight):
    inputs = frames.reshape(-1, E).astype(jnp.float32)
    normed = layer_norm(inputs, ln_gain.astype(jnp.float32), ln_bias.astype(jnp.float32)).astype(jnp.bfloat16)
    raised = jnp.dot(normed, enc_up, preferred_element_type=jnp.float32) + up_bias.astype(jnp.float32)
    active_units = jax.nn.gelu(raised, approximate=False).astype(jnp.bfloat16)
    lowered = jnp.dot(active_units, enc_down, preferred_element_type=jnp.float32)
    encoded = (inputs + lowered + down_bias.astype(jnp.float32)).astype(jnp.bfloat16)
    stacked = encoded.reshape(-1, D_A)
    lifted = jax.nn.gelu(jnp.dot(stacked, adapt_in, preferred_element_type=jnp.float32), approximate=False).astype(jnp.bfloat16)
    adapted = jnp.dot(lifted, adapt_out, preferred_element_type=jnp.float32).astype(jnp.bfloat16)
    adapted = adapted.reshape(N_POOL, N_SECTION, GR, D)
    tables = jax.vmap(jax.vmap(lambda route_row, length_row: slot_tables(route_row, length_row, N_POOL, CAPW)))
    starts, span_rows = tables(routes[..., 0], lengths)
    starts = jnp.transpose(starts, (2, 1, 0, 3))
    span_rows = jnp.transpose(span_rows, (2, 1, 0, 3))
    offsets = jnp.arange(WIN_MAX, dtype=jnp.int32)
    row_valid = offsets < span_rows[..., None]
    row_index = jnp.where(row_valid, starts[..., None] + offsets, 0).astype(jnp.int32)
    pool_ids = jnp.arange(N_POOL, dtype=jnp.int32)[None, None, :, None, None]
    section_ids = jnp.arange(N_SECTION, dtype=jnp.int32)[None, :, None, None, None]
    gathered = adapted[pool_ids, section_ids, row_index]
    sequences = jnp.where(row_valid[..., None], gathered, jnp.zeros_like(gathered))
    seq_count = N_POOL * N_SECTION
    slot_count = N_POOL * CAPW
    hidden_rows = sequences.reshape(seq_count, SEQ, D).astype(jnp.float32)
    key_ok = row_valid.reshape(seq_count, slot_count, WIN_MAX)
    causal = offsets[:, None] >= offsets[None, :]
    allowed = causal[None, None] & key_ok[:, :, None, :]
    group_size = HQ // HK
    share_cols = QD // N_TP
    for layer_index in range(LAYERS):
        current = hidden_rows
        normed_rows = rms_norm(current, attn_gain[layer_index].astype(jnp.float32)).astype(jnp.bfloat16).reshape(-1, D)
        queries = jnp.dot(normed_rows, q_weight[layer_index], preferred_element_type=jnp.float32).astype(jnp.bfloat16)
        queries = queries.reshape(seq_count, slot_count, WIN_MAX, HK, group_size, HD)
        key_rows = jnp.dot(normed_rows, k_weight[layer_index], preferred_element_type=jnp.float32).astype(jnp.bfloat16)
        key_rows = key_rows.reshape(seq_count, slot_count, WIN_MAX, HK, HD)
        values = jnp.dot(normed_rows, v_weight[layer_index], preferred_element_type=jnp.float32).astype(jnp.bfloat16)
        values = values.reshape(seq_count, slot_count, WIN_MAX, HK, HD)
        scores = jnp.einsum('nswkgd,nsukd->nskgwu', queries.astype(jnp.float32), key_rows.astype(jnp.float32)) * HD ** (-0.5)
        scores = jnp.where(allowed[:, :, None, None], scores, -1e+30)
        row_max = lax.optimization_barrier(jnp.max(scores, axis=-1, keepdims=True))
        exponent = jnp.exp(scores - row_max)
        weights = (exponent / lax.optimization_barrier(jnp.sum(exponent, axis=-1, keepdims=True))).astype(jnp.bfloat16)
        context = jnp.einsum('nskgwu,nsukd->nswkgd', weights.astype(jnp.float32), values.astype(jnp.float32)).astype(jnp.bfloat16)
        context = context.reshape(-1, QD)
        summed = jnp.zeros((context.shape[0], D), jnp.float32)
        for group_index in range(N_TP):
            low = group_index * share_cols
            head_term = jnp.dot(context[:, low:low + share_cols], o_weight[layer_index, low:low + share_cols], preferred_element_type=jnp.float32).astype(jnp.bfloat16)
            summed = summed + lax.optimization_barrier(head_term).astype(jnp.float32)
        updated = current + summed.reshape(seq_count, SEQ, D)
        if layer_index < LAYERS - 1:
            updated = lax.optimization_barrier(updated.astype(jnp.bfloat16)).astype(jnp.float32)
        hidden_rows = updated
    row_ok = key_ok.reshape(seq_count, SEQ, 1)
    decoded = jnp.where(row_ok, hidden_rows, jnp.zeros_like(hidden_rows))
    return decoded.reshape(N_POOL, N_SECTION, SEQ, D)
```

```python
import jax
import jax.numpy as jnp
from jax import lax
from jax.sharding import PartitionSpec as P

HD = 128
WIN_MAX = 16
CAPW = 2
STACK = 4
EPSILON = 1e-05
BF = jnp.bfloat16
F32 = jnp.float32


def layer_norm(values, gain_row, shift_row):
    mean_value = jnp.mean(values, axis=-1, keepdims=True)
    centered = values - mean_value
    variance = jnp.mean(centered * centered, axis=-1, keepdims=True)
    return centered * lax.rsqrt(variance + EPSILON) * gain_row + shift_row


def slot_tables(route_row, length_row, dest_count, capacity):
    windows = route_row.shape[0]
    window_ids = jnp.arange(windows, dtype=jnp.int32)
    starts = jnp.cumsum(length_row, dtype=jnp.int32) - length_row
    earlier = (route_row[None, :] == route_row[:, None]) & (
        window_ids[None, :] < window_ids[:, None]
    )
    window_rank = jnp.sum(earlier.astype(jnp.int32), axis=1, dtype=jnp.int32)
    dest_ids = jnp.arange(dest_count, dtype=jnp.int32)
    rank_ids = jnp.arange(capacity, dtype=jnp.int32)
    chosen = (route_row[None, None, :] == dest_ids[:, None, None]) & (
        window_rank[None, None, :] == rank_ids[None, :, None]
    )
    chosen = chosen.astype(jnp.int32)
    return (
        jnp.sum(chosen * starts, axis=2, dtype=jnp.int32),
        jnp.sum(chosen * length_row, axis=2, dtype=jnp.int32),
    )


def dot(a, b):
    return jnp.dot(a, b, preferred_element_type=F32)


def per_device(
    frames,
    ln_gain,
    ln_bias,
    enc_up,
    up_bias,
    enc_down,
    down_bias,
    adapt_in,
    adapt_out,
    lengths,
    routes,
    attn_gain,
    q_weight,
    k_weight,
    v_weight,
    o_weight,
):
    pool_count = lax.axis_size("pool")
    tp_count = lax.axis_size("tp")
    section_count = lax.axis_size("section")
    z_count = tp_count // 2
    pool_index = lax.axis_index("pool")
    section_index = lax.axis_index("section")
    tp_index = lax.axis_index("tp")
    y_low = tp_index % 2
    core = section_index % 2
    high = section_index // 2
    z_groups = [[2 * z + y for z in range(z_count)] for y in range(2)]
    y_pairs = [(i, i ^ 1) for i in range(tp_count)]

    def chip_swap(value):
        return lax.ppermute(value, "section", [(i, i ^ 1) for i in range(section_count)])

    def y_swap(value):
        return lax.ppermute(value, "tp", y_pairs)

    def z_all_to_all(value):
        return lax.all_to_all(
            value, "tp", split_axis=0, concat_axis=0, tiled=True, axis_index_groups=z_groups
        )

    def ordered(index, own, other):
        return jnp.where(index == 0, jnp.stack([own, other]), jnp.stack([other, own]))

    def scatter_sum(partial):
        arrived = z_all_to_all(partial)
        summed = jnp.sum(arrived.astype(F32), axis=0)
        half = summed.shape[1] // 2
        kept = lax.dynamic_slice_in_dim(summed, y_low * half, half, 1)
        sent = lax.dynamic_slice_in_dim(summed, (1 - y_low) * half, half, 1).astype(BF)
        return kept + y_swap(sent).astype(F32)

    def gather_blocks(shard):
        pair = ordered(y_low, shard, y_swap(shard))
        spread = jnp.broadcast_to(pair[None], (z_count,) + pair.shape)
        blocks = z_all_to_all(spread)
        rows = shard.shape[0]
        return jnp.transpose(blocks, (2, 0, 1, 3)).reshape(rows, -1)

    def to_blocks(partial):
        rows = partial.shape[0]
        return jnp.transpose(
            partial.astype(BF).reshape(rows, z_count, -1), (1, 0, 2)
        )

    own_layer = (attn_gain[0], q_weight[0], k_weight[0], v_weight[0], o_weight[0])
    other_layer = tuple(chip_swap(weight) for weight in own_layer)
    other_in, other_out = chip_swap(adapt_in), chip_swap(adapt_out)

    width = frames.shape[3]
    tokens = frames.shape[2] // STACK
    inputs = jnp.transpose(frames[0, 0].reshape(tokens, STACK, width), (1, 0, 2))
    inputs = inputs.reshape(STACK * tokens, width).astype(F32)
    normed = layer_norm(inputs, ln_gain.astype(F32), ln_bias.astype(F32)).astype(BF)
    raised = dot(normed, enc_up) + up_bias.astype(F32)
    active_units = jax.nn.gelu(raised, approximate=False).astype(BF)
    partial_down = dot(active_units, enc_down).astype(BF).reshape(STACK, tokens, width)
    summed_down = scatter_sum(partial_down)
    half = width // 2
    own_inputs = lax.dynamic_slice(
        inputs, ((tp_index // 2) * tokens, y_low * half), (tokens, half)
    )
    own_bias = lax.dynamic_slice_in_dim(down_bias, y_low * half, half, 0).astype(F32)
    encoded = (own_inputs + summed_down + own_bias).astype(BF)

    swapped = lax.ppermute(encoded, "section", [(i, i ^ 2) for i in range(section_count)])
    both = ordered(high, encoded, swapped).reshape(2 * tokens, -1)
    stacked = gather_blocks(both)
    partial_out = sum(
        dot(jax.nn.gelu(dot(stacked, w_in), approximate=False).astype(BF), w_out)
        for w_in, w_out in ((adapt_in, adapt_out), (other_in, other_out))
    )
    half_sum = scatter_sum(to_blocks(partial_out))
    from_high = lax.ppermute(half_sum.astype(BF), "section", [(2, 0), (3, 1)])
    hidden = (half_sum + from_high.astype(F32)).astype(BF)

    ends = jnp.cumsum(lengths[pool_index], axis=1, dtype=jnp.int32)
    token_ids = jnp.arange(tokens, dtype=jnp.int32)
    windows = jnp.sum(
        (ends[:, None, :] <= token_ids[None, :, None]).astype(jnp.int32), axis=2, dtype=jnp.int32
    )
    tags = windows + jnp.arange(section_count, dtype=jnp.int32)[:, None] * lengths.shape[2]
    tags = lax.dynamic_slice_in_dim(tags.reshape(2, 2, tokens), core, 1, 1).reshape(-1)
    row_ids = jnp.arange(2 * tokens, dtype=jnp.int32)
    allowed = (tags[:, None] == tags[None, :]) & (row_ids[None, :] <= row_ids[:, None])

    def attend(rows, weights):
        gain, wq, wk, wv, wo = weights
        values = rows.astype(F32)
        normed_rows = (
            values
            * lax.rsqrt(jnp.mean(values * values, axis=-1, keepdims=True) + EPSILON)
            * gain.astype(F32)
        ).astype(BF)
        count = rows.shape[0]
        queries = dot(normed_rows, wq).astype(BF).reshape(count, -1, HD)
        keys = dot(normed_rows, wk).astype(BF)
        vals = dot(normed_rows, wv).astype(BF)
        scores = jnp.einsum("whd,ud->hwu", queries, keys, preferred_element_type=F32) * HD ** (
            -0.5
        )
        scores = jnp.where(allowed[None], scores, -1e30)
        exponent = jnp.exp(scores - jnp.max(scores, axis=-1, keepdims=True))
        probs = (exponent / jnp.sum(exponent, axis=-1, keepdims=True)).astype(BF)
        context = jnp.einsum("hwu,ud->whd", probs, vals, preferred_element_type=F32).astype(BF)
        return to_blocks(dot(context.reshape(count, -1), wo))

    for turn in range(4):
        rows = gather_blocks(hidden)
        partial = lax.cond(
            core == turn % 2,
            lambda: attend(rows, own_layer),
            lambda: attend(rows, other_layer),
        )
        updated = hidden.astype(F32) + scatter_sum(partial)
        hidden = updated.astype(BF)
        if turn == 1:
            hidden = lax.ppermute(hidden, "section", [(0, 2), (1, 3)])

    to_low = lax.ppermute(hidden[:tokens], "section", [(2, 0), (3, 1)])
    final = jnp.where(high == 0, to_low, hidden[tokens:])
    tables = jax.vmap(
        jax.vmap(lambda route_row, length_row: slot_tables(route_row, length_row, pool_count, CAPW))
    )
    starts, spans = tables(routes[..., 0], lengths)
    offsets = jnp.arange(WIN_MAX, dtype=jnp.int32)
    row_valid = offsets < spans[pool_index, section_index][..., None]
    row_index = jnp.where(row_valid, starts[pool_index, section_index][..., None] + offsets, 0)
    picked = jnp.take(final, row_index.reshape(-1), axis=0)
    outgoing = jnp.where(row_valid.reshape(-1, 1), picked, jnp.zeros_like(picked))
    outgoing = outgoing.reshape(pool_count, CAPW * WIN_MAX, -1)
    incoming = lax.all_to_all(outgoing, "pool", split_axis=0, concat_axis=0, tiled=True)
    incoming = incoming.reshape(tp_count, WIN_MAX, -1)
    landed = lax.all_to_all(incoming, "tp", split_axis=0, concat_axis=0, tiled=True)
    decoded = jnp.transpose(landed, (1, 0, 2)).reshape(WIN_MAX, -1).astype(F32)
    return decoded[None, None]


def solution(mesh):
    in_specs = (
        P("pool", "section", None, None),
        P(),
        P(),
        P(None, "tp"),
        P("tp"),
        P("tp", None),
        P(),
        P(None, ("section", "tp")),
        P(("section", "tp"), None),
        P(),
        P(),
        P("section", None),
        P("section", None, "tp"),
        P("section", None, "tp"),
        P("section", None, "tp"),
        P("section", "tp", None),
    )
    out_specs = P("pool", "section", "tp", None)
    return jax.shard_map(
        per_device, mesh=mesh, in_specs=in_specs, out_specs=out_specs, check_vma=False
    )
```

```python
import jax
import jax.numpy as jnp
from jax import lax
from jax.experimental import pallas as pl
from jax.experimental.pallas import tpu as pltpu
from jax.sharding import PartitionSpec as P

HD = 128
LANES = 128
WIN_MAX = 16
CAPW = 2
STACK = 4
EPSILON = 1e-05
BF = jnp.bfloat16
F32 = jnp.float32


def slot_tables(route_row, length_row, dest_count, capacity):
    windows = route_row.shape[0]
    window_ids = jnp.arange(windows, dtype=jnp.int32)
    starts = jnp.cumsum(length_row, dtype=jnp.int32) - length_row
    earlier = (route_row[None, :] == route_row[:, None]) & (
        window_ids[None, :] < window_ids[:, None]
    )
    window_rank = jnp.sum(earlier.astype(jnp.int32), axis=1, dtype=jnp.int32)
    dest_ids = jnp.arange(dest_count, dtype=jnp.int32)
    rank_ids = jnp.arange(capacity, dtype=jnp.int32)
    chosen = (route_row[None, None, :] == dest_ids[:, None, None]) & (
        window_rank[None, None, :] == rank_ids[None, :, None]
    )
    chosen = chosen.astype(jnp.int32)
    return (
        jnp.sum(chosen * starts, axis=2, dtype=jnp.int32),
        jnp.sum(chosen * length_row, axis=2, dtype=jnp.int32),
    )


def dot(a, b):
    return jnp.dot(a, b, preferred_element_type=F32)

def exact_gelu(x):
    return 0.5 * x * (1.0 + lax.erf(x * (0.5**0.5)))


def vmem():
    return pl.BlockSpec(memory_space=pltpu.VMEM)


def anywhere():
    return pl.BlockSpec(memory_space=pl.ANY)


def smem():
    return pl.BlockSpec(memory_space=pltpu.SMEM)


def encoder_kernel(
    frames_ref, gain_ref, bias_ref, up_ref, up_bias_ref, down_ref, out_ref, up_v, down_v, rows, sems
):
    copies = [
        pltpu.make_async_copy(up_ref, up_v, sems.at[0]),
        pltpu.make_async_copy(down_ref, down_v, sems.at[1]),
    ]
    for copy in copies:
        copy.start()
    values = frames_ref[...].astype(F32)
    centered = values - jnp.mean(values, axis=-1, keepdims=True)
    variance = jnp.mean(centered * centered, axis=-1, keepdims=True)
    normed = (
        centered * lax.rsqrt(variance + EPSILON) * gain_ref[...].astype(F32)
        + bias_ref[...].astype(F32)
    ).astype(BF)
    copies[0].wait()
    raised = dot(normed, up_v[...]) + up_bias_ref[...].astype(F32)
    active = exact_gelu(raised).astype(BF)
    copies[1].wait()
    lowered = dot(active, down_v[...])
    group, count = out_ref.shape[0], out_ref.shape[1]
    for c in range(rows.shape[0]):
        cols = slice(c * LANES, (c + 1) * LANES)
        rows[c] = lowered[:, cols]
        for j in range(group):
            out_ref[j, :, cols] = rows[c, pl.ds(j, count, stride=group), :].astype(BF)


def encoder(frames, gain, bias, up, up_bias, down):
    count, width = frames.shape
    hidden = up.shape[1]
    return pl.pallas_call(
        encoder_kernel,
        out_shape=jax.ShapeDtypeStruct((STACK, count // STACK, width), BF),
        in_specs=[vmem(), vmem(), vmem(), anywhere(), vmem(), anywhere()],
        out_specs=vmem(),
        scratch_shapes=[
            pltpu.VMEM((width, hidden), BF),
            pltpu.VMEM((hidden, width), BF),
            pltpu.VMEM((width // LANES, count, LANES), F32),
            pltpu.SemaphoreType.DMA((2,)),
        ],
        compiler_params=pltpu.CompilerParams(vmem_limit_bytes=32 << 20),
        cost_estimate=pl.CostEstimate(
            flops=4 * count * width * hidden,
            bytes_accessed=4 * width * hidden,
            transcendentals=count * hidden,
        ),
        name="encoder_units",
    )(frames, gain.reshape(1, -1), bias.reshape(1, -1), up, up_bias.reshape(1, -1), down)


def adapter_kernel(x_ref, in0, in1, out0, out1, part_ref, win, wout, sems):
    in_copies = [
        pltpu.make_async_copy(ref, win.at[i], sems.at[i]) for i, ref in enumerate((in0, in1))
    ]
    out_copies = [
        pltpu.make_async_copy(ref, wout.at[i], sems.at[2 + i])
        for i, ref in enumerate((out0, out1))
    ]
    for copy in in_copies + out_copies:
        copy.start()
    blocks, _, depth = x_ref.shape
    lifted = []
    for i in range(2):
        in_copies[i].wait()
        total = sum(
            dot(x_ref[b], win[i, b * depth : (b + 1) * depth, :]) for b in range(blocks)
        )
        lifted.append(exact_gelu(total).astype(BF))
    for copy in out_copies:
        copy.wait()
    for b in range(blocks):
        cols = slice(b * depth, (b + 1) * depth)
        part_ref[b] = sum(dot(lifted[i], wout[i, :, cols]) for i in range(2)).astype(BF)


def adapter(blocks, in_pair, out_pair):
    width, units = in_pair[0].shape
    rows = blocks.shape[1]
    return pl.pallas_call(
        adapter_kernel,
        out_shape=jax.ShapeDtypeStruct(blocks.shape, BF),
        in_specs=[vmem()] + [anywhere()] * 4,
        out_specs=vmem(),
        scratch_shapes=[
            pltpu.VMEM((2, width, units), BF),
            pltpu.VMEM((2, units, width), BF),
            pltpu.SemaphoreType.DMA((4,)),
        ],
        compiler_params=pltpu.CompilerParams(vmem_limit_bytes=40 << 20),
        cost_estimate=pl.CostEstimate(
            flops=8 * rows * width * units,
            bytes_accessed=8 * width * units,
            transcendentals=2 * rows * units,
        ),
        name="adapter_units",
    )(blocks, *in_pair, *out_pair)


def layer_kernel(
    which, x_ref, gain_ref, mask_ref, q0, k0, v0, o0, q1, k1, v1, o1, out_ref, wq, wk, wv, wo, sems
):
    blocks, rows, depth = x_ref.shape

    def copies(q_ref, k_ref, v_ref, o_ref):
        made = []
        for b in range(blocks):
            part = pl.ds(b * depth, depth)
            made.append(
                [
                    pltpu.make_async_copy(q_ref.at[part, :], wq.at[b], sems.at[0, b]),
                    pltpu.make_async_copy(k_ref.at[part, :], wk.at[b], sems.at[1, b]),
                    pltpu.make_async_copy(v_ref.at[part, :], wv.at[b], sems.at[2, b]),
                    pltpu.make_async_copy(o_ref.at[:, part], wo.at[b], sems.at[3, b]),
                ]
            )
        return made

    def begin(refs):
        made = copies(*refs)
        for group in made:
            for copy in group[:3]:
                copy.start()
        for group in made:
            group[3].start()

    @pl.when(which[0] == 0)
    def _():
        begin((q0, k0, v0, o0))

    @pl.when(which[0] != 0)
    def _():
        begin((q1, k1, v1, o1))

    waits = copies(q0, k0, v0, o0)
    squares = sum(
        jnp.sum(jnp.square(x_ref[b].astype(F32)), axis=-1, keepdims=True) for b in range(blocks)
    )
    scale = lax.rsqrt(squares / (blocks * depth) + EPSILON)
    queries, keys, values = 0.0, 0.0, 0.0
    for b in range(blocks):
        gain = gain_ref[:, b * depth : (b + 1) * depth].astype(F32)
        normed = (x_ref[b].astype(F32) * scale * gain).astype(BF)
        for copy in waits[b][:3]:
            copy.wait()
        queries += dot(normed, wq[b])
        keys += dot(normed, wk[b])
        values += dot(normed, wv[b])
    heads = queries.shape[1] // HD
    queries = queries.astype(BF)
    stacked = jnp.concatenate([queries[:, h * HD : (h + 1) * HD] for h in range(heads)], axis=0)
    scores = lax.dot_general(
        stacked, keys.astype(BF), (((1,), (1,)), ((), ())), preferred_element_type=F32
    ) * HD ** (-0.5)
    mask = jnp.concatenate([mask_ref[...]] * heads, axis=0)
    scores = jnp.where(mask > 0.5, scores, -1e30)
    exponent = jnp.exp(scores - jnp.max(scores, axis=-1, keepdims=True))
    probs = (exponent / jnp.sum(exponent, axis=-1, keepdims=True)).astype(BF)
    context = dot(probs, values.astype(BF)).astype(BF)
    context = jnp.concatenate([context[h * rows : (h + 1) * rows] for h in range(heads)], axis=1)
    for b in range(blocks):
        waits[b][3].wait()
        out_ref[b] = dot(context, wo[b]).astype(BF)


def decoder_layer(which, blocks, gain, mask, own, other):
    count, rows, depth = blocks.shape
    q_cols, kv_cols = own[0].shape[1], own[1].shape[1]
    weights = count * depth * (2 * q_cols + 2 * kv_cols)
    return pl.pallas_call(
        layer_kernel,
        out_shape=jax.ShapeDtypeStruct(blocks.shape, BF),
        in_specs=[smem(), vmem(), vmem(), vmem()] + [anywhere()] * 8,
        out_specs=vmem(),
        scratch_shapes=[
            pltpu.VMEM((count, depth, q_cols), BF),
            pltpu.VMEM((count, depth, kv_cols), BF),
            pltpu.VMEM((count, depth, kv_cols), BF),
            pltpu.VMEM((count, q_cols, depth), BF),
            pltpu.SemaphoreType.DMA((4, count)),
        ],
        compiler_params=pltpu.CompilerParams(vmem_limit_bytes=40 << 20),
        cost_estimate=pl.CostEstimate(
            flops=2 * rows * weights, bytes_accessed=2 * weights, transcendentals=rows * rows * 4
        ),
        name="decoder_layer",
    )(which, blocks, gain.reshape(1, -1), mask, *own, *other)


def per_device(
    frames,
    ln_gain,
    ln_bias,
    enc_up,
    up_bias,
    enc_down,
    down_bias,
    adapt_in,
    adapt_out,
    lengths,
    routes,
    attn_gain,
    q_weight,
    k_weight,
    v_weight,
    o_weight,
):
    pool_count = lax.axis_size("pool")
    tp_count = lax.axis_size("tp")
    section_count = lax.axis_size("section")
    z_count = tp_count // 2
    pool_index = lax.axis_index("pool")
    section_index = lax.axis_index("section")
    tp_index = lax.axis_index("tp")
    z_index, y_low = tp_index // 2, tp_index % 2
    core, high = section_index % 2, section_index // 2
    z_groups = [[2 * z + y for z in range(z_count)] for y in range(2)]

    def chip_swap(value):
        return lax.ppermute(value, "section", [(i, i ^ 1) for i in range(section_count)])

    def y_move(value, moves):
        pairs = []
        for high_from, high_to, y_flip in moves:
            for c in range(2):
                for t in range(tp_count):
                    pairs.append(
                        (
                            (2 * high_from + c) * tp_count + t,
                            (2 * high_to + c) * tp_count + (t ^ y_flip),
                        )
                    )
        return lax.ppermute(value, ("section", "tp"), pairs)

    def z_all_to_all(value):
        return lax.all_to_all(
            value, "tp", split_axis=0, concat_axis=0, tiled=True, axis_index_groups=z_groups
        )

    def z_sum(partial):
        return jnp.sum(z_all_to_all(partial).astype(F32), axis=0)

    def z_gather(shard):
        return z_all_to_all(jnp.broadcast_to(shard[None], (z_count,) + shard.shape))

    def at_first(value):
        return jnp.where(y_low == 0, value, jnp.zeros_like(value))

    both = ((0, 0, 1), (1, 1, 1))

    own_layer = (q_weight[0], k_weight[0], v_weight[0], o_weight[0])
    other_layer = tuple(chip_swap(weight) for weight in own_layer)
    own_gain, other_gain = attn_gain[0], chip_swap(attn_gain[0])
    in_pair = (adapt_in, chip_swap(adapt_in))
    out_pair = (adapt_out, chip_swap(adapt_out))

    width = frames.shape[3]
    tokens = frames.shape[2] // STACK
    partial_down = encoder(frames[0, 0], ln_gain, ln_bias, enc_up, up_bias, enc_down)
    own_frames = lax.dynamic_index_in_dim(
        frames[0, 0].reshape(tokens, STACK, width), z_index, 1, keepdims=False
    )
    extra = at_first(own_frames.astype(F32) + down_bias.astype(F32)[None])
    share = (z_sum(partial_down) + extra).astype(BF)
    here = share.astype(F32) + y_move(share, both).astype(F32)
    there = y_move(share, ((0, 1, 0), (1, 0, 0))).astype(F32) + y_move(
        share, ((0, 1, 1), (1, 0, 1))
    ).astype(F32)
    encoded = jnp.where(high == 0, jnp.stack([here, there]), jnp.stack([there, here]))
    encoded = encoded.astype(BF).reshape(2 * tokens, width)

    share = z_sum(adapter(z_gather(encoded), in_pair, out_pair)).astype(BF)
    moved = (
        y_move(share, both),
        y_move(share, ((1, 0, 0),)),
        y_move(share, ((1, 0, 1),)),
    )
    hidden = (share.astype(F32) + sum(part.astype(F32) for part in moved)).astype(BF)

    ends = jnp.cumsum(lengths[pool_index], axis=1, dtype=jnp.int32)
    token_ids = jnp.arange(tokens, dtype=jnp.int32)
    windows = jnp.sum(
        (ends[:, None, :] <= token_ids[None, :, None]).astype(jnp.int32), axis=2, dtype=jnp.int32
    )
    tags = windows + jnp.arange(section_count, dtype=jnp.int32)[:, None] * lengths.shape[2]
    tags = lax.dynamic_slice_in_dim(tags.reshape(2, 2, tokens), core, 1, 1).reshape(-1)
    row_ids = jnp.arange(2 * tokens, dtype=jnp.int32)
    allowed = (tags[:, None] == tags[None, :]) & (row_ids[None, :] <= row_ids[:, None])
    mask = allowed.astype(F32)

    tables = jax.vmap(
        jax.vmap(lambda route_row, length_row: slot_tables(route_row, length_row, pool_count, CAPW))
    )
    starts, spans = tables(routes[..., 0], lengths)
    offsets = jnp.arange(WIN_MAX, dtype=jnp.int32)

    def of_pair(table):
        pair = lax.dynamic_index_in_dim(table, pool_index, 0, keepdims=False)
        pair = pair.reshape((2, 2) + pair.shape[1:])
        pair = lax.dynamic_index_in_dim(pair, core, 1, keepdims=False)
        return jnp.transpose(pair, (0, 2, 1))

    row_valid = offsets < of_pair(spans)[..., None]
    row_index = of_pair(starts)[..., None] + offsets
    row_index = row_index + (jnp.arange(2, dtype=jnp.int32) * tokens)[:, None, None, None]
    row_index = jnp.where(row_valid, row_index, 0)

    for turn in range(4):
        which = (core != turn % 2).astype(jnp.int32)
        gain = jnp.where(which == 0, own_gain, other_gain)
        partial = decoder_layer(
            which.reshape(1), z_gather(hidden), gain, mask, own_layer, other_layer
        )
        share = (z_sum(partial) + at_first(hidden.astype(F32))).astype(BF)
        if turn == 1:
            moved = (y_move(share, ((0, 1, 0),)), y_move(share, ((0, 1, 1),)))
            hidden = sum(part.astype(F32) for part in moved).astype(BF)
        elif turn < 3:
            hidden = (share.astype(F32) + y_move(share, both).astype(F32)).astype(BF)

    picked = jnp.take(share, row_index.reshape(-1), axis=0)
    picked = jnp.where(row_valid.reshape(-1, 1), picked, jnp.zeros_like(picked))
    picked = picked.reshape(2, CAPW, pool_count, WIN_MAX, width)
    stay = lax.dynamic_index_in_dim(picked, y_low, 1, keepdims=False)
    leave = lax.dynamic_index_in_dim(picked, 1 - y_low, 1, keepdims=False)
    moved = (
        y_move(stay[0], ((1, 0, 0),)),
        y_move(leave[0], ((1, 0, 1),)),
        y_move(leave[1], ((1, 1, 1),)),
        jnp.where(high == 1, stay[1], jnp.zeros_like(stay[1])),
    )
    final = sum(part.astype(F32) for part in moved).astype(BF)
    landed = []
    for step in range(pool_count):
        pairs = []
        for x in range(pool_count):
            for z in range(z_count):
                for y in range(2):
                    pairs.append(
                        (
                            x * tp_count + 2 * z + y,
                            ((z + step) % pool_count) * tp_count + 2 * x + y,
                        )
                    )
        piece = lax.dynamic_index_in_dim(
            final, (z_index + step) % pool_count, 0, keepdims=False
        )
        landed.append(lax.ppermute(piece, ("pool", "tp"), pairs))
    landed = jnp.stack(landed)
    blocks = [
        lax.dynamic_index_in_dim(landed, (pool_index - z) % pool_count, 0, keepdims=False)
        for z in range(z_count)
    ]
    decoded = jnp.concatenate(blocks, axis=1).astype(F32)
    return decoded[None, None]


def solution(mesh):
    in_specs = (
        P("pool", "section", None, None),
        P(),
        P(),
        P(None, "tp"),
        P("tp"),
        P("tp", None),
        P(),
        P(None, ("section", "tp")),
        P(("section", "tp"), None),
        P(),
        P(),
        P("section", None),
        P("section", None, "tp"),
        P("section", None, "tp"),
        P("section", None, "tp"),
        P("section", "tp", None),
    )
    out_specs = P("pool", "section", "tp", None)
    return jax.shard_map(
        per_device, mesh=mesh, in_specs=in_specs, out_specs=out_specs, check_vma=False
    )
```

```python
import jax
import jax.numpy as jnp
from jax import lax
from jax.experimental import pallas as pl
from jax.experimental.pallas import tpu as pltpu
from jax.sharding import PartitionSpec as P

HD = 128
LANES = 128
WIN_MAX = 16
CAPW = 2
STACK = 4
EPSILON = 1e-05
BF = jnp.bfloat16
F32 = jnp.float32


def slot_tables(route_row, length_row, dest_count, capacity):
    windows = route_row.shape[0]
    window_ids = jnp.arange(windows, dtype=jnp.int32)
    starts = jnp.cumsum(length_row, dtype=jnp.int32) - length_row
    earlier = (route_row[None, :] == route_row[:, None]) & (
        window_ids[None, :] < window_ids[:, None]
    )
    window_rank = jnp.sum(earlier.astype(jnp.int32), axis=1, dtype=jnp.int32)
    dest_ids = jnp.arange(dest_count, dtype=jnp.int32)
    rank_ids = jnp.arange(capacity, dtype=jnp.int32)
    chosen = (route_row[None, None, :] == dest_ids[:, None, None]) & (
        window_rank[None, None, :] == rank_ids[None, :, None]
    )
    chosen = chosen.astype(jnp.int32)
    return (
        jnp.sum(chosen * starts, axis=2, dtype=jnp.int32),
        jnp.sum(chosen * length_row, axis=2, dtype=jnp.int32),
    )


def dot(a, b):
    return jnp.dot(a, b, preferred_element_type=F32)

def dot_t(a, b):
    return lax.dot_general(a, b, (((1,), (1,)), ((), ())), preferred_element_type=F32)


def exact_gelu(x):
    return 0.5 * x * (1.0 + lax.erf(x * (0.5**0.5)))


def vmem():
    return pl.BlockSpec(memory_space=pltpu.VMEM)


def anywhere():
    return pl.BlockSpec(memory_space=pl.ANY)


def smem():
    return pl.BlockSpec(memory_space=pltpu.SMEM)


def encoder_kernel(
    frames_ref, gain_ref, bias_ref, up_ref, up_bias_ref, down_ref, out_ref, up_v, down_v, rows, sems
):
    copies = [
        pltpu.make_async_copy(up_ref, up_v, sems.at[0]),
        pltpu.make_async_copy(down_ref, down_v, sems.at[1]),
    ]
    for copy in copies:
        copy.start()
    values = frames_ref[...].astype(F32)
    centered = values - jnp.mean(values, axis=-1, keepdims=True)
    variance = jnp.mean(centered * centered, axis=-1, keepdims=True)
    normed = (
        centered * lax.rsqrt(variance + EPSILON) * gain_ref[...].astype(F32)[None]
        + bias_ref[...].astype(F32)[None]
    ).astype(BF)
    copies[0].wait()
    raised = dot(normed, up_v[...]) + up_bias_ref[...].astype(F32)[None]
    active = exact_gelu(raised).astype(BF)
    copies[1].wait()
    lowered = dot(active, down_v[...])
    group, count = out_ref.shape[0], out_ref.shape[1]
    for c in range(rows.shape[0]):
        cols = slice(c * LANES, (c + 1) * LANES)
        rows[c] = lowered[:, cols]
        for j in range(group):
            out_ref[j, :, cols] = rows[c, pl.ds(j, count, stride=group), :].astype(BF)


def encoder(frames, gain, bias, up, up_bias, down):
    count, width = frames.shape
    hidden = up.shape[1]
    return pl.pallas_call(
        encoder_kernel,
        out_shape=jax.ShapeDtypeStruct((STACK, count // STACK, width), BF),
        in_specs=[vmem(), vmem(), vmem(), anywhere(), vmem(), anywhere()],
        out_specs=vmem(),
        scratch_shapes=[
            pltpu.VMEM((width, hidden), BF),
            pltpu.VMEM((hidden, width), BF),
            pltpu.VMEM((width // LANES, count, LANES), F32),
            pltpu.SemaphoreType.DMA((2,)),
        ],
        compiler_params=pltpu.CompilerParams(vmem_limit_bytes=56 << 20),
        cost_estimate=pl.CostEstimate(
            flops=4 * count * width * hidden,
            bytes_accessed=4 * width * hidden,
            transcendentals=count * hidden,
        ),
        name="encoder_units",
    )(frames, gain, bias, up, up_bias, down)


def adapter_kernel(x_ref, in0, in1, out0, out1, part_ref, win, wout, sems):
    in_copies = [
        pltpu.make_async_copy(ref, win.at[i], sems.at[i]) for i, ref in enumerate((in0, in1))
    ]
    out_copies = [
        pltpu.make_async_copy(ref, wout.at[i], sems.at[2 + i])
        for i, ref in enumerate((out0, out1))
    ]
    for copy in in_copies + out_copies:
        copy.start()
    blocks, _, depth = x_ref.shape
    lifted = []
    for i in range(2):
        in_copies[i].wait()
        total = sum(
            dot_t(x_ref[b], win[i, :, b * depth : (b + 1) * depth]) for b in range(blocks)
        )
        lifted.append(exact_gelu(total).astype(BF))
    for copy in out_copies:
        copy.wait()
    for b in range(blocks):
        cols = slice(b * depth, (b + 1) * depth)
        part_ref[b] = sum(dot(lifted[i], wout[i, :, cols]) for i in range(2)).astype(BF)


def adapter(blocks, in_pair, out_pair):
    units, width = in_pair[0].shape
    rows = blocks.shape[1]
    return pl.pallas_call(
        adapter_kernel,
        out_shape=jax.ShapeDtypeStruct(blocks.shape, BF),
        in_specs=[vmem()] + [anywhere()] * 4,
        out_specs=vmem(),
        scratch_shapes=[
            pltpu.VMEM((2, units, width), BF),
            pltpu.VMEM((2, units, width), BF),
            pltpu.SemaphoreType.DMA((4,)),
        ],
        compiler_params=pltpu.CompilerParams(vmem_limit_bytes=56 << 20),
        cost_estimate=pl.CostEstimate(
            flops=8 * rows * width * units,
            bytes_accessed=8 * width * units,
            transcendentals=2 * rows * units,
        ),
        name="adapter_units",
    )(blocks, *in_pair, *out_pair)


def layer_kernel(
    which, x_ref, gain0, gain1, mask_ref, q0, k0, v0, o0, q1, k1, v1, o1, out_ref, wq, wk, wv, wo, sems
):
    blocks, rows, depth = x_ref.shape

    def copies(q_ref, k_ref, v_ref, o_ref):
        made = []
        for b in range(blocks):
            part = pl.ds(b * depth, depth)
            made.append(
                [
                    pltpu.make_async_copy(q_ref.at[part, :], wq.at[b], sems.at[0, b]),
                    pltpu.make_async_copy(k_ref.at[part, :], wk.at[b], sems.at[1, b]),
                    pltpu.make_async_copy(v_ref.at[part, :], wv.at[b], sems.at[2, b]),
                    pltpu.make_async_copy(o_ref.at[:, part], wo.at[b], sems.at[3, b]),
                ]
            )
        return made

    def begin(refs):
        made = copies(*refs)
        for group in made:
            for copy in group[:3]:
                copy.start()
        for group in made:
            group[3].start()

    @pl.when(which[0] == 0)
    def _():
        begin((q0, k0, v0, o0))

    @pl.when(which[0] != 0)
    def _():
        begin((q1, k1, v1, o1))

    waits = copies(q0, k0, v0, o0)
    squares = sum(
        jnp.sum(jnp.square(x_ref[b].astype(F32)), axis=-1, keepdims=True) for b in range(blocks)
    )
    scale = lax.rsqrt(squares / (blocks * depth) + EPSILON)
    queries, keys, values = 0.0, 0.0, 0.0
    for b in range(blocks):
        cols = slice(b * depth, (b + 1) * depth)
        gain = jnp.where(which[0] == 0, gain0[:, cols], gain1[:, cols])
        normed = (x_ref[b].astype(F32) * scale * gain).astype(BF)
        for copy in waits[b][:3]:
            copy.wait()
        queries += dot(normed, wq[b])
        keys += dot(normed, wk[b])
        values += dot(normed, wv[b])
    heads = queries.shape[1] // HD
    queries = queries.astype(BF)
    stacked = jnp.concatenate([queries[:, h * HD : (h + 1) * HD] for h in range(heads)], axis=0)
    scores = dot_t(stacked, keys.astype(BF)) * HD ** (-0.5)
    mask = jnp.concatenate([mask_ref[...]] * heads, axis=0)
    scores = jnp.where(mask > 0.5, scores, -1e30)
    exponent = jnp.exp(scores - jnp.max(scores, axis=-1, keepdims=True))
    probs = (exponent / jnp.sum(exponent, axis=-1, keepdims=True)).astype(BF)
    context = dot(probs, values.astype(BF)).astype(BF)
    context = jnp.concatenate([context[h * rows : (h + 1) * rows] for h in range(heads)], axis=1)
    for b in range(blocks):
        waits[b][3].wait()
        out_ref[b] = dot(context, wo[b]).astype(BF)


def decoder_layer(which, blocks, gains, mask, own, other):
    count, rows, depth = blocks.shape
    q_cols, kv_cols = own[0].shape[1], own[1].shape[1]
    weights = count * depth * (2 * q_cols + 2 * kv_cols)
    return pl.pallas_call(
        layer_kernel,
        out_shape=jax.ShapeDtypeStruct(blocks.shape, BF),
        in_specs=[smem(), vmem(), vmem(), vmem(), vmem()] + [anywhere()] * 8,
        out_specs=vmem(),
        scratch_shapes=[
            pltpu.VMEM((count, depth, q_cols), BF),
            pltpu.VMEM((count, depth, kv_cols), BF),
            pltpu.VMEM((count, depth, kv_cols), BF),
            pltpu.VMEM((count, q_cols, depth), BF),
            pltpu.SemaphoreType.DMA((4, count)),
        ],
        compiler_params=pltpu.CompilerParams(vmem_limit_bytes=56 << 20),
        cost_estimate=pl.CostEstimate(
            flops=2 * rows * weights, bytes_accessed=2 * weights, transcendentals=rows * rows * 4
        ),
        name="decoder_layer",
    )(which, blocks, *gains, mask, *own, *other)


def per_device(
    frames,
    ln_gain,
    ln_bias,
    enc_up,
    up_bias,
    enc_down,
    down_bias,
    adapt_in,
    adapt_out,
    lengths,
    routes,
    attn_gain,
    q_weight,
    k_weight,
    v_weight,
    o_weight,
):
    pool_count = lax.axis_size("pool")
    tp_count = lax.axis_size("tp")
    section_count = lax.axis_size("section")
    z_count = tp_count // 2
    pool_index = lax.axis_index("pool")
    section_index = lax.axis_index("section")
    tp_index = lax.axis_index("tp")
    z_index, y_low = tp_index // 2, tp_index % 2
    core, high = section_index % 2, section_index // 2
    z_groups = [[2 * z + y for z in range(z_count)] for y in range(2)]

    def chip_swap(value):
        return lax.ppermute(value, "section", [(i, i ^ 1) for i in range(section_count)])

    def y_move(value, moves):
        pairs = []
        for high_from, high_to, y_flip in moves:
            for c in range(2):
                for t in range(tp_count):
                    pairs.append(
                        (
                            (2 * high_from + c) * tp_count + t,
                            (2 * high_to + c) * tp_count + (t ^ y_flip),
                        )
                    )
        return lax.ppermute(value, ("section", "tp"), pairs)

    def z_all_to_all(value):
        return lax.all_to_all(
            value, "tp", split_axis=0, concat_axis=0, tiled=True, axis_index_groups=z_groups
        )

    def z_sum(partial):
        return jnp.sum(z_all_to_all(partial).astype(F32), axis=0)

    def z_gather(shard):
        return z_all_to_all(jnp.broadcast_to(shard[None], (z_count,) + shard.shape))

    def at_first(value):
        return jnp.where(y_low == 0, value, jnp.zeros_like(value))

    both = ((0, 0, 1), (1, 1, 1))

    own_layer = (q_weight[0], k_weight[0], v_weight[0], o_weight[0])
    other_layer = tuple(chip_swap(weight) for weight in own_layer)
    gains = [g.astype(F32).reshape(1, -1) for g in (attn_gain[0], chip_swap(attn_gain[0]))]
    in_pair = (adapt_in.T, chip_swap(adapt_in.T))
    out_pair = (adapt_out, chip_swap(adapt_out))

    width = frames.shape[3]
    tokens = frames.shape[2] // STACK
    partial_down = encoder(frames[0, 0], ln_gain, ln_bias, enc_up, up_bias, enc_down)
    own_frames = lax.dynamic_index_in_dim(
        frames[0, 0].reshape(tokens, STACK, width), z_index, 1, keepdims=False
    )
    extra = at_first(own_frames.astype(F32) + down_bias.astype(F32)[None])
    share = (z_sum(partial_down) + extra).astype(BF)
    here = share.astype(F32) + y_move(share, both).astype(F32)
    there = y_move(share, ((0, 1, 0), (1, 0, 0))).astype(F32) + y_move(
        share, ((0, 1, 1), (1, 0, 1))
    ).astype(F32)
    here, in_pair, out_pair, other_layer, gains = lax.optimization_barrier(
        (here, in_pair, out_pair, other_layer, gains)
    )
    encoded = jnp.where(high == 0, jnp.stack([here, there]), jnp.stack([there, here]))
    encoded = encoded.astype(BF).reshape(2 * tokens, width)

    share = z_sum(adapter(z_gather(encoded), in_pair, out_pair)).astype(BF)
    moved = (
        y_move(share, both),
        y_move(share, ((1, 0, 0),)),
        y_move(share, ((1, 0, 1),)),
    )
    hidden = (share.astype(F32) + sum(part.astype(F32) for part in moved)).astype(BF)

    ends = jnp.cumsum(lengths[pool_index], axis=1, dtype=jnp.int32)
    token_ids = jnp.arange(tokens, dtype=jnp.int32)
    windows = jnp.sum(
        (ends[:, None, :] <= token_ids[None, :, None]).astype(jnp.int32), axis=2, dtype=jnp.int32
    )
    tags = windows + jnp.arange(section_count, dtype=jnp.int32)[:, None] * lengths.shape[2]
    tags = lax.dynamic_slice_in_dim(tags.reshape(2, 2, tokens), core, 1, 1).reshape(-1)
    row_ids = jnp.arange(2 * tokens, dtype=jnp.int32)
    allowed = (tags[:, None] == tags[None, :]) & (row_ids[None, :] <= row_ids[:, None])
    mask = allowed.astype(F32)

    tables = jax.vmap(
        jax.vmap(lambda route_row, length_row: slot_tables(route_row, length_row, pool_count, CAPW))
    )
    starts, spans = tables(routes[..., 0], lengths)
    offsets = jnp.arange(WIN_MAX, dtype=jnp.int32)

    def of_pair(table):
        pair = lax.dynamic_index_in_dim(table, pool_index, 0, keepdims=False)
        pair = pair.reshape((2, 2) + pair.shape[1:])
        pair = lax.dynamic_index_in_dim(pair, core, 1, keepdims=False)
        return jnp.transpose(pair, (0, 2, 1))

    row_valid = offsets < of_pair(spans)[..., None]
    row_index = of_pair(starts)[..., None] + offsets
    row_index = row_index + (jnp.arange(2, dtype=jnp.int32) * tokens)[:, None, None, None]
    row_index = jnp.where(row_valid, row_index, 0)

    for turn in range(4):
        which = (core != turn % 2).astype(jnp.int32)
        partial = decoder_layer(
            which.reshape(1), z_gather(hidden), gains, mask, own_layer, other_layer
        )
        share = (z_sum(partial) + at_first(hidden.astype(F32))).astype(BF)
        if turn == 1:
            moved = (y_move(share, ((0, 1, 0),)), y_move(share, ((0, 1, 1),)))
            hidden = sum(part.astype(F32) for part in moved).astype(BF)
        elif turn < 3:
            hidden = (share.astype(F32) + y_move(share, both).astype(F32)).astype(BF)

    picked = jnp.take(share, row_index.reshape(-1), axis=0)
    picked = jnp.where(row_valid.reshape(-1, 1), picked, jnp.zeros_like(picked))
    picked = picked.reshape(2, CAPW, pool_count, WIN_MAX, width)
    stay = lax.dynamic_index_in_dim(picked, y_low, 1, keepdims=False)
    leave = lax.dynamic_index_in_dim(picked, 1 - y_low, 1, keepdims=False)
    moved = (
        y_move(stay[0], ((1, 0, 0),)),
        y_move(leave[0], ((1, 0, 1),)),
        y_move(leave[1], ((1, 1, 1),)),
        jnp.where(high == 1, stay[1], jnp.zeros_like(stay[1])),
    )
    final = sum(part.astype(F32) for part in moved).astype(BF)
    landed = []
    for step in range(pool_count):
        pairs = []
        for x in range(pool_count):
            for z in range(z_count):
                for y in range(2):
                    pairs.append(
                        (
                            x * tp_count + 2 * z + y,
                            ((z + step) % pool_count) * tp_count + 2 * x + y,
                        )
                    )
        piece = lax.dynamic_index_in_dim(
            final, (z_index + step) % pool_count, 0, keepdims=False
        )
        landed.append(lax.ppermute(piece, ("pool", "tp"), pairs))
    landed = jnp.stack(landed)
    blocks = [
        lax.dynamic_index_in_dim(landed, (pool_index - z) % pool_count, 0, keepdims=False)
        for z in range(z_count)
    ]
    decoded = jnp.concatenate(blocks, axis=1).astype(F32)
    return decoded[None, None]


def solution(mesh):
    in_specs = (
        P("pool", "section", None, None),
        P(),
        P(),
        P(None, "tp"),
        P("tp"),
        P("tp", None),
        P(),
        P(None, ("section", "tp")),
        P(("section", "tp"), None),
        P(),
        P(),
        P("section", None),
        P("section", None, "tp"),
        P("section", None, "tp"),
        P("section", None, "tp"),
        P("section", "tp", None),
    )
    out_specs = P("pool", "section", "tp", None)
    return jax.shard_map(
        per_device, mesh=mesh, in_specs=in_specs, out_specs=out_specs, check_vma=False
    )
```

```python
import jax
import jax.numpy as jnp
from jax import lax
from jax.experimental import pallas as pl
from jax.experimental.pallas import tpu as pltpu
from jax.sharding import PartitionSpec as P

HD = 128
LANES = 128
WIN_MAX = 16
CAPW = 2
STACK = 4
EPSILON = 1e-05
BF = jnp.bfloat16
F32 = jnp.float32


def slot_tables(route_row, length_row, dest_count, capacity):
    windows = route_row.shape[0]
    window_ids = jnp.arange(windows, dtype=jnp.int32)
    starts = jnp.cumsum(length_row, dtype=jnp.int32) - length_row
    earlier = (route_row[None, :] == route_row[:, None]) & (
        window_ids[None, :] < window_ids[:, None]
    )
    window_rank = jnp.sum(earlier.astype(jnp.int32), axis=1, dtype=jnp.int32)
    dest_ids = jnp.arange(dest_count, dtype=jnp.int32)
    rank_ids = jnp.arange(capacity, dtype=jnp.int32)
    chosen = (route_row[None, None, :] == dest_ids[:, None, None]) & (
        window_rank[None, None, :] == rank_ids[None, :, None]
    )
    chosen = chosen.astype(jnp.int32)
    return (
        jnp.sum(chosen * starts, axis=2, dtype=jnp.int32),
        jnp.sum(chosen * length_row, axis=2, dtype=jnp.int32),
    )


def dot(a, b):
    return jnp.dot(a, b, preferred_element_type=F32)

def dot_t(a, b):
    return lax.dot_general(a, b, (((1,), (1,)), ((), ())), preferred_element_type=F32)


def exact_gelu(x):
    return 0.5 * x * (1.0 + lax.erf(x * (0.5**0.5)))


def vmem():
    return pl.BlockSpec(memory_space=pltpu.VMEM)


def anywhere():
    return pl.BlockSpec(memory_space=pl.ANY)


def smem():
    return pl.BlockSpec(memory_space=pltpu.SMEM)


def block_at(index, depth):
    return pl.ds(pl.multiple_of(index * depth, depth), depth)


def encoder_kernel(place, frames_ref, gain_ref, bias_ref, up_ref, up_bias_ref, down_ref, *rest):
    outs, (up_v, down_v, rows, sems) = rest[:STACK], rest[STACK:]
    copies = [
        pltpu.make_async_copy(up_ref, up_v, sems.at[0]),
        pltpu.make_async_copy(down_ref, down_v, sems.at[1]),
    ]
    for copy in copies:
        copy.start()
    values = frames_ref[...].astype(F32)
    centered = values - jnp.mean(values, axis=-1, keepdims=True)
    variance = jnp.mean(centered * centered, axis=-1, keepdims=True)
    normed = (
        centered * lax.rsqrt(variance + EPSILON) * gain_ref[...].astype(F32)[None]
        + bias_ref[...].astype(F32)[None]
    ).astype(BF)
    copies[0].wait()
    raised = dot(normed, up_v[...]) + up_bias_ref[...].astype(F32)[None]
    active = exact_gelu(raised).astype(BF)
    copies[1].wait()
    lowered = dot(active, down_v[...])
    count = outs[0].shape[0]
    for c in range(rows.shape[0]):
        cols = slice(c * LANES, (c + 1) * LANES)
        rows[c] = lowered[:, cols]
        for step in range(STACK):
            j = lax.rem(place[0] + step, STACK)
            outs[step][:, cols] = rows[c, pl.ds(j, count, stride=STACK), :].astype(BF)


def encoder(place, frames, gain, bias, up, up_bias, down):
    count, width = frames.shape
    hidden = up.shape[1]
    return pl.pallas_call(
        encoder_kernel,
        out_shape=[jax.ShapeDtypeStruct((count // STACK, width), BF)] * STACK,
        in_specs=[smem(), vmem(), vmem(), vmem(), anywhere(), vmem(), anywhere()],
        out_specs=[vmem()] * STACK,
        scratch_shapes=[
            pltpu.VMEM((width, hidden), BF),
            pltpu.VMEM((hidden, width), BF),
            pltpu.VMEM((width // LANES, count, LANES), F32),
            pltpu.SemaphoreType.DMA((2,)),
        ],
        compiler_params=pltpu.CompilerParams(vmem_limit_bytes=56 << 20),
        cost_estimate=pl.CostEstimate(
            flops=4 * count * width * hidden,
            bytes_accessed=4 * width * hidden,
            transcendentals=count * hidden,
        ),
        name="encoder_units",
    )(place, frames, gain, bias, up, up_bias, down)


def adapter_kernel(place, x0, x1, x2, x3, in0, in1, out0, out1, *rest):
    xs, outs, (win, wout, sems) = (x0, x1, x2, x3), rest[:4], rest[4:]
    blocks, depth = len(xs), x0.shape[1]
    units = in0.shape[0]
    made = [[], []]
    for k in range(blocks):
        sources = lax.rem(place[0] + blocks - k, blocks), lax.rem(place[0] + k, blocks)
        for kind, pair in enumerate(((in0, in1), (out0, out1))):
            part = block_at(sources[kind], depth)
            for i in range(2):
                target = (win, wout)[kind].at[k, pl.ds(i * units, units), :]
                made[kind].append(
                    pltpu.make_async_copy(pair[i].at[:, part], target, sems.at[kind, i, k])
                )
    for copy in made[0] + made[1]:
        copy.start()
    total = 0.0
    for k in range(blocks):
        for copy in made[0][2 * k : 2 * k + 2]:
            copy.wait()
        total += dot_t(xs[k][...], win[k])
    lifted = exact_gelu(total).astype(BF)
    for k in range(blocks):
        for copy in made[1][2 * k : 2 * k + 2]:
            copy.wait()
        outs[k][...] = dot(lifted, wout[k]).astype(BF)


def adapter(place, blocks, in_pair, out_pair):
    units, width = in_pair[0].shape
    count, (rows, depth) = len(blocks), blocks[0].shape
    return pl.pallas_call(
        adapter_kernel,
        out_shape=[jax.ShapeDtypeStruct((rows, depth), BF)] * count,
        in_specs=[smem()] + [vmem()] * count + [anywhere()] * 4,
        out_specs=[vmem()] * count,
        scratch_shapes=[
            pltpu.VMEM((count, 2 * units, depth), BF),
            pltpu.VMEM((count, 2 * units, depth), BF),
            pltpu.SemaphoreType.DMA((2, 2, count)),
        ],
        compiler_params=pltpu.CompilerParams(vmem_limit_bytes=56 << 20),
        cost_estimate=pl.CostEstimate(
            flops=8 * rows * width * units,
            bytes_accessed=8 * width * units,
            transcendentals=2 * rows * units,
        ),
        name="adapter_units",
    )(place, *blocks, *in_pair, *out_pair)


def layer_kernel(
    which, x_hbm, gain0, gain1, mask_ref, q0, k0, v0, o0, q1, k1, v1, o1, out_ref, x_ref, wq, wk, wv, wo, sems
):
    blocks, rows, depth = x_ref.shape
    x_copies = [
        pltpu.make_async_copy(x_hbm.at[b], x_ref.at[b], sems.at[4, b]) for b in range(blocks)
    ]
    for copy in x_copies:
        copy.start()

    def copies(q_ref, k_ref, v_ref, o_ref):
        made = []
        for b in range(blocks):
            part = pl.ds(b * depth, depth)
            made.append(
                [
                    pltpu.make_async_copy(q_ref.at[part, :], wq.at[b], sems.at[0, b]),
                    pltpu.make_async_copy(k_ref.at[part, :], wk.at[b], sems.at[1, b]),
                    pltpu.make_async_copy(v_ref.at[part, :], wv.at[b], sems.at[2, b]),
                    pltpu.make_async_copy(o_ref.at[:, part], wo.at[b], sems.at[3, b]),
                ]
            )
        return made

    def begin(refs):
        made = copies(*refs)
        for group in made:
            for copy in group[:3]:
                copy.start()
        for group in made:
            group[3].start()

    @pl.when(which[0] == 0)
    def _():
        begin((q0, k0, v0, o0))

    @pl.when(which[0] != 0)
    def _():
        begin((q1, k1, v1, o1))

    waits = copies(q0, k0, v0, o0)
    for copy in x_copies:
        copy.wait()
    squares = sum(
        jnp.sum(jnp.square(x_ref[b].astype(F32)), axis=-1, keepdims=True) for b in range(blocks)
    )
    scale = lax.rsqrt(squares / (blocks * depth) + EPSILON)
    queries, keys, values = 0.0, 0.0, 0.0
    for b in range(blocks):
        cols = slice(b * depth, (b + 1) * depth)
        gain = jnp.where(which[0] == 0, gain0[:, cols], gain1[:, cols])
        normed = (x_ref[b].astype(F32) * scale * gain).astype(BF)
        for copy in waits[b][:3]:
            copy.wait()
        queries += dot(normed, wq[b])
        keys += dot(normed, wk[b])
        values += dot(normed, wv[b])
    heads = queries.shape[1] // HD
    queries = queries.astype(BF)
    stacked = jnp.concatenate([queries[:, h * HD : (h + 1) * HD] for h in range(heads)], axis=0)
    scores = dot_t(stacked, keys.astype(BF)) * HD ** (-0.5)
    mask = jnp.concatenate([mask_ref[...]] * heads, axis=0)
    scores = jnp.where(mask > 0.5, scores, -1e30)
    exponent = jnp.exp(scores - jnp.max(scores, axis=-1, keepdims=True))
    probs = (exponent / jnp.sum(exponent, axis=-1, keepdims=True)).astype(BF)
    context = dot(probs, values.astype(BF)).astype(BF)
    context = jnp.concatenate([context[h * rows : (h + 1) * rows] for h in range(heads)], axis=1)
    for b in range(blocks):
        waits[b][3].wait()
        out_ref[b] = dot(context, wo[b]).astype(BF)


def decoder_layer(which, blocks, gains, mask, own, other):
    count, rows, depth = blocks.shape
    q_cols, kv_cols = own[0].shape[1], own[1].shape[1]
    weights = count * depth * (2 * q_cols + 2 * kv_cols)
    return pl.pallas_call(
        layer_kernel,
        out_shape=jax.ShapeDtypeStruct(blocks.shape, BF),
        in_specs=[smem(), anywhere(), vmem(), vmem(), vmem()] + [anywhere()] * 8,
        out_specs=vmem(),
        scratch_shapes=[
            pltpu.VMEM(blocks.shape, BF),
            pltpu.VMEM((count, depth, q_cols), BF),
            pltpu.VMEM((count, depth, kv_cols), BF),
            pltpu.VMEM((count, depth, kv_cols), BF),
            pltpu.VMEM((count, q_cols, depth), BF),
            pltpu.SemaphoreType.DMA((5, count)),
        ],
        compiler_params=pltpu.CompilerParams(vmem_limit_bytes=56 << 20),
        cost_estimate=pl.CostEstimate(
            flops=2 * rows * weights, bytes_accessed=2 * weights, transcendentals=rows * rows * 4
        ),
        name="decoder_layer",
    )(which, blocks, *gains, mask, *own, *other)


def per_device(
    frames,
    ln_gain,
    ln_bias,
    enc_up,
    up_bias,
    enc_down,
    down_bias,
    adapt_in,
    adapt_out,
    lengths,
    routes,
    attn_gain,
    q_weight,
    k_weight,
    v_weight,
    o_weight,
):
    pool_count = lax.axis_size("pool")
    tp_count = lax.axis_size("tp")
    section_count = lax.axis_size("section")
    z_count = tp_count // 2
    pool_index = lax.axis_index("pool")
    section_index = lax.axis_index("section")
    tp_index = lax.axis_index("tp")
    z_index, y_low = tp_index // 2, tp_index % 2
    core, high = section_index % 2, section_index // 2
    z_groups = [[2 * z + y for z in range(z_count)] for y in range(2)]

    def chip_swap(value):
        return lax.ppermute(value, "section", [(i, i ^ 1) for i in range(section_count)])

    def y_move(value, moves):
        pairs = []
        for high_from, high_to, y_flip in moves:
            for c in range(2):
                for t in range(tp_count):
                    pairs.append(
                        (
                            (2 * high_from + c) * tp_count + t,
                            (2 * high_to + c) * tp_count + (t ^ y_flip),
                        )
                    )
        return lax.ppermute(value, ("section", "tp"), pairs)

    def z_all_to_all(value):
        return lax.all_to_all(
            value, "tp", split_axis=0, concat_axis=0, tiled=True, axis_index_groups=z_groups
        )

    def z_sum(partial):
        return jnp.sum(z_all_to_all(partial).astype(F32), axis=0)

    def z_move(value, step):
        pairs = [
            (2 * z + y, 2 * ((z + step) % z_count) + y) for z in range(z_count) for y in range(2)
        ]
        return lax.ppermute(value, "tp", pairs)

    def z_scatter(parts):
        moved = [z_move(parts[step], step) for step in range(1, z_count)]
        return sum(part.astype(F32) for part in [parts[0]] + moved)

    def z_spread(shard):
        return [shard] + [z_move(shard, step) for step in range(1, z_count)]

    def z_gather(shard):
        return z_all_to_all(jnp.broadcast_to(shard[None], (z_count,) + shard.shape))

    def at_first(value):
        return jnp.where(y_low == 0, value, jnp.zeros_like(value))

    both = ((0, 0, 1), (1, 1, 1))

    own_layer = (q_weight[0], k_weight[0], v_weight[0], o_weight[0])
    early = [chip_swap(own_layer[0]), chip_swap(own_layer[3])]
    in_pair = (adapt_in.T, chip_swap(adapt_in.T))
    out_pair = (adapt_out, chip_swap(adapt_out))

    width = frames.shape[3]
    tokens = frames.shape[2] // STACK
    place = z_index.astype(jnp.int32).reshape(1)
    partial_down = encoder(place, frames[0, 0], ln_gain, ln_bias, enc_up, up_bias, enc_down)
    own_frames = lax.dynamic_index_in_dim(
        frames[0, 0].reshape(tokens, STACK, width), z_index, 1, keepdims=False
    )
    extra = at_first(own_frames.astype(F32) + down_bias.astype(F32)[None])
    share = (z_scatter(partial_down) + extra).astype(BF)
    here = (share.astype(F32) + y_move(share, both).astype(F32)).astype(BF)
    here, in_pair, out_pair, early, own_layer = lax.optimization_barrier(
        (here, in_pair, out_pair, early, own_layer)
    )
    gains = [g.astype(F32).reshape(1, -1) for g in (attn_gain[0], chip_swap(attn_gain[0]))]
    other_layer = (early[0], chip_swap(own_layer[1]), chip_swap(own_layer[2]), early[1])
    there = y_move(here, ((0, 1, 1), (1, 0, 1)))
    encoded = jnp.where(high == 0, jnp.stack([here, there]), jnp.stack([there, here]))
    encoded = encoded.reshape(2 * tokens, width)

    share = z_scatter(adapter(place, z_spread(encoded), in_pair, out_pair)).astype(BF)
    summed = share.astype(F32) + y_move(share, both).astype(F32)
    from_high = y_move(summed.astype(BF), ((1, 0, 1),))
    hidden = (summed + from_high.astype(F32)).astype(BF)

    ends = jnp.cumsum(lengths[pool_index], axis=1, dtype=jnp.int32)
    token_ids = jnp.arange(tokens, dtype=jnp.int32)
    windows = jnp.sum(
        (ends[:, None, :] <= token_ids[None, :, None]).astype(jnp.int32), axis=2, dtype=jnp.int32
    )
    tags = windows + jnp.arange(section_count, dtype=jnp.int32)[:, None] * lengths.shape[2]
    tags = lax.dynamic_slice_in_dim(tags.reshape(2, 2, tokens), core, 1, 1).reshape(-1)
    row_ids = jnp.arange(2 * tokens, dtype=jnp.int32)
    allowed = (tags[:, None] == tags[None, :]) & (row_ids[None, :] <= row_ids[:, None])
    mask = allowed.astype(F32)

    tables = jax.vmap(
        jax.vmap(lambda route_row, length_row: slot_tables(route_row, length_row, pool_count, CAPW))
    )
    starts, spans = tables(routes[..., 0], lengths)
    offsets = jnp.arange(WIN_MAX, dtype=jnp.int32)

    def of_pair(table):
        pair = lax.dynamic_index_in_dim(table, pool_index, 0, keepdims=False)
        pair = pair.reshape((2, 2) + pair.shape[1:])
        pair = lax.dynamic_index_in_dim(pair, core, 1, keepdims=False)
        return jnp.transpose(pair, (0, 2, 1))

    row_valid = offsets < of_pair(spans)[..., None]
    row_index = of_pair(starts)[..., None] + offsets
    row_index = row_index + (jnp.arange(2, dtype=jnp.int32) * tokens)[:, None, None, None]
    row_index = jnp.where(row_valid, row_index, 0)

    for turn in range(4):
        which = (core != turn % 2).astype(jnp.int32)
        partial = decoder_layer(
            which.reshape(1), z_gather(hidden), gains, mask, own_layer, other_layer
        )
        share = (z_sum(partial) + at_first(hidden.astype(F32))).astype(BF)
        if turn == 1:
            moved = (y_move(share, ((0, 1, 0),)), y_move(share, ((0, 1, 1),)))
            hidden = sum(part.astype(F32) for part in moved).astype(BF)
        elif turn < 3:
            hidden = (share.astype(F32) + y_move(share, both).astype(F32)).astype(BF)

    picked = jnp.take(share, row_index.reshape(-1), axis=0)
    picked = jnp.where(row_valid.reshape(-1, 1), picked, jnp.zeros_like(picked))
    picked = picked.reshape(2, CAPW, pool_count, WIN_MAX, width)
    stay = lax.dynamic_index_in_dim(picked, y_low, 1, keepdims=False)
    leave = lax.dynamic_index_in_dim(picked, 1 - y_low, 1, keepdims=False)
    moved = (
        y_move(stay[0], ((1, 0, 0),)),
        y_move(leave[0], ((1, 0, 1),)),
        y_move(leave[1], ((1, 1, 1),)),
        jnp.where(high == 1, stay[1], jnp.zeros_like(stay[1])),
    )
    final = sum(part.astype(F32) for part in moved).astype(BF)
    landed = []
    for step in range(pool_count):
        pairs = []
        for x in range(pool_count):
            for z in range(z_count):
                for y in range(2):
                    pairs.append(
                        (
                            x * tp_count + 2 * z + y,
                            ((z + step) % pool_count) * tp_count + 2 * x + y,
                        )
                    )
        piece = lax.dynamic_index_in_dim(
            final, (z_index + step) % pool_count, 0, keepdims=False
        )
        landed.append(lax.ppermute(piece, ("pool", "tp"), pairs))
    landed = jnp.stack(landed)
    blocks = [
        lax.dynamic_index_in_dim(landed, (pool_index - z) % pool_count, 0, keepdims=False)
        for z in range(z_count)
    ]
    decoded = jnp.concatenate(blocks, axis=1).astype(F32)
    return decoded[None, None]


def solution(mesh):
    in_specs = (
        P("pool", "section", None, None),
        P(),
        P(),
        P(None, "tp"),
        P("tp"),
        P("tp", None),
        P(),
        P(None, ("section", "tp")),
        P(("section", "tp"), None),
        P(),
        P(),
        P("section", None),
        P("section", None, "tp"),
        P("section", None, "tp"),
        P("section", None, "tp"),
        P("section", "tp", None),
    )
    out_specs = P("pool", "section", "tp", None)
    return jax.shard_map(
        per_device, mesh=mesh, in_specs=in_specs, out_specs=out_specs, check_vma=False
    )
```

```python
import jax
import jax.numpy as jnp
from jax import lax
from jax.experimental import pallas as pl
from jax.experimental.pallas import tpu as pltpu
from jax.sharding import PartitionSpec as P

HD = 128
LANES = 128
WIN_MAX = 16
CAPW = 2
STACK = 4
EPSILON = 1e-05
BF = jnp.bfloat16
F32 = jnp.float32


def slot_tables(route_row, length_row, dest_count, capacity):
    windows = route_row.shape[0]
    window_ids = jnp.arange(windows, dtype=jnp.int32)
    starts = jnp.cumsum(length_row, dtype=jnp.int32) - length_row
    earlier = (route_row[None, :] == route_row[:, None]) & (
        window_ids[None, :] < window_ids[:, None]
    )
    window_rank = jnp.sum(earlier.astype(jnp.int32), axis=1, dtype=jnp.int32)
    dest_ids = jnp.arange(dest_count, dtype=jnp.int32)
    rank_ids = jnp.arange(capacity, dtype=jnp.int32)
    chosen = (route_row[None, None, :] == dest_ids[:, None, None]) & (
        window_rank[None, None, :] == rank_ids[None, :, None]
    )
    chosen = chosen.astype(jnp.int32)
    return (
        jnp.sum(chosen * starts, axis=2, dtype=jnp.int32),
        jnp.sum(chosen * length_row, axis=2, dtype=jnp.int32),
    )


def dot(a, b):
    return jnp.dot(a, b, preferred_element_type=F32)

def dot_t(a, b):
    return lax.dot_general(a, b, (((1,), (1,)), ((), ())), preferred_element_type=F32)


def exact_gelu(x):
    return 0.5 * x * (1.0 + lax.erf(x * (0.5**0.5)))


def vmem():
    return pl.BlockSpec(memory_space=pltpu.VMEM)


def anywhere():
    return pl.BlockSpec(memory_space=pl.ANY)


def smem():
    return pl.BlockSpec(memory_space=pltpu.SMEM)


def block_at(index, depth):
    return pl.ds(pl.multiple_of(index * depth, depth), depth)


def encoder_kernel(place, frames_ref, gain_ref, bias_ref, up_ref, up_bias_ref, down_ref, *rest):
    outs, (up_v, down_v, rows, sems) = rest[:STACK], rest[STACK:]
    copies = [
        pltpu.make_async_copy(up_ref, up_v, sems.at[0]),
        pltpu.make_async_copy(down_ref, down_v, sems.at[1]),
    ]
    for copy in copies:
        copy.start()
    values = frames_ref[...].astype(F32)
    centered = values - jnp.mean(values, axis=-1, keepdims=True)
    variance = jnp.mean(centered * centered, axis=-1, keepdims=True)
    normed = (
        centered * lax.rsqrt(variance + EPSILON) * gain_ref[...].astype(F32)[None]
        + bias_ref[...].astype(F32)[None]
    ).astype(BF)
    copies[0].wait()
    raised = dot(normed, up_v[...]) + up_bias_ref[...].astype(F32)[None]
    active = exact_gelu(raised).astype(BF)
    copies[1].wait()
    lowered = dot(active, down_v[...])
    count = outs[0].shape[0]
    for c in range(rows.shape[0]):
        cols = slice(c * LANES, (c + 1) * LANES)
        rows[c] = lowered[:, cols]
        for step in range(STACK):
            j = lax.rem(place[0] + place[1] * step, STACK)
            outs[step][:, cols] = rows[c, pl.ds(j, count, stride=STACK), :].astype(BF)


def encoder(place, frames, gain, bias, up, up_bias, down):
    count, width = frames.shape
    hidden = up.shape[1]
    return pl.pallas_call(
        encoder_kernel,
        out_shape=[jax.ShapeDtypeStruct((count // STACK, width), BF)] * STACK,
        in_specs=[smem(), vmem(), vmem(), vmem(), anywhere(), vmem(), anywhere()],
        out_specs=[vmem()] * STACK,
        scratch_shapes=[
            pltpu.VMEM((width, hidden), BF),
            pltpu.VMEM((hidden, width), BF),
            pltpu.VMEM((width // LANES, count, LANES), F32),
            pltpu.SemaphoreType.DMA((2,)),
        ],
        compiler_params=pltpu.CompilerParams(vmem_limit_bytes=56 << 20),
        cost_estimate=pl.CostEstimate(
            flops=4 * count * width * hidden,
            bytes_accessed=4 * width * hidden,
            transcendentals=count * hidden,
        ),
        name="encoder_units",
    )(place, frames, gain, bias, up, up_bias, down)


def adapter_kernel(place, x0, x1, x2, x3, in0, in1, out0, out1, *rest):
    xs, outs, (win, wout, sems) = (x0, x1, x2, x3), rest[:4], rest[4:]
    blocks, depth = len(xs), x0.shape[1]
    units = in0.shape[0]
    made = [[], []]
    for k in range(blocks):
        away = place[1] * k
        sources = (
            lax.rem(place[0] + blocks * blocks - away, blocks),
            lax.rem(place[0] + away, blocks),
        )
        for kind, pair in enumerate(((in0, in1), (out0, out1))):
            part = block_at(sources[kind], depth)
            for i in range(2):
                target = (win, wout)[kind].at[k, pl.ds(i * units, units), :]
                made[kind].append(
                    pltpu.make_async_copy(pair[i].at[:, part], target, sems.at[kind, i, k])
                )
    for copy in made[0] + made[1]:
        copy.start()
    total = 0.0
    for k in range(blocks):
        for copy in made[0][2 * k : 2 * k + 2]:
            copy.wait()
        total += dot_t(xs[k][...], win[k])
    lifted = exact_gelu(total).astype(BF)
    for k in range(blocks):
        for copy in made[1][2 * k : 2 * k + 2]:
            copy.wait()
        outs[k][...] = dot(lifted, wout[k]).astype(BF)


def adapter(place, blocks, in_pair, out_pair):
    units, width = in_pair[0].shape
    count, (rows, depth) = len(blocks), blocks[0].shape
    return pl.pallas_call(
        adapter_kernel,
        out_shape=[jax.ShapeDtypeStruct((rows, depth), BF)] * count,
        in_specs=[smem()] + [vmem()] * count + [anywhere()] * 4,
        out_specs=[vmem()] * count,
        scratch_shapes=[
            pltpu.VMEM((count, 2 * units, depth), BF),
            pltpu.VMEM((count, 2 * units, depth), BF),
            pltpu.SemaphoreType.DMA((2, 2, count)),
        ],
        compiler_params=pltpu.CompilerParams(vmem_limit_bytes=32 << 20),
        cost_estimate=pl.CostEstimate(
            flops=8 * rows * width * units,
            bytes_accessed=8 * width * units,
            transcendentals=2 * rows * units,
        ),
        name="adapter_units",
    )(place, *blocks, *in_pair, *out_pair)


def layer_kernel(
    which, x_hbm, gain0, gain1, mask_ref, q0, k0, v0, o0, q1, k1, v1, o1, out_ref, x_ref, wq, wk, wv, wo, sems
):
    blocks, rows, depth = x_ref.shape
    x_copies = [
        pltpu.make_async_copy(x_hbm.at[b], x_ref.at[b], sems.at[4, b]) for b in range(blocks)
    ]
    for copy in x_copies:
        copy.start()

    def copies(q_ref, k_ref, v_ref, o_ref):
        made = []
        for b in range(blocks):
            part = pl.ds(b * depth, depth)
            made.append(
                [
                    pltpu.make_async_copy(q_ref.at[part, :], wq.at[b], sems.at[0, b]),
                    pltpu.make_async_copy(k_ref.at[part, :], wk.at[b], sems.at[1, b]),
                    pltpu.make_async_copy(v_ref.at[part, :], wv.at[b], sems.at[2, b]),
                    pltpu.make_async_copy(o_ref.at[:, part], wo.at[b], sems.at[3, b]),
                ]
            )
        return made

    def begin(refs):
        made = copies(*refs)
        for group in made:
            for copy in group[:3]:
                copy.start()
        for group in made:
            group[3].start()

    @pl.when(which[0] == 0)
    def _():
        begin((q0, k0, v0, o0))

    @pl.when(which[0] != 0)
    def _():
        begin((q1, k1, v1, o1))

    waits = copies(q0, k0, v0, o0)
    for copy in x_copies:
        copy.wait()
    squares = sum(
        jnp.sum(jnp.square(x_ref[b].astype(F32)), axis=-1, keepdims=True) for b in range(blocks)
    )
    scale = lax.rsqrt(squares / (blocks * depth) + EPSILON)
    queries, keys, values = 0.0, 0.0, 0.0
    for b in range(blocks):
        cols = slice(b * depth, (b + 1) * depth)
        gain = jnp.where(which[0] == 0, gain0[:, cols], gain1[:, cols])
        normed = (x_ref[b].astype(F32) * scale * gain).astype(BF)
        for copy in waits[b][:3]:
            copy.wait()
        queries += dot(normed, wq[b])
        keys += dot(normed, wk[b])
        values += dot(normed, wv[b])
    heads = queries.shape[1] // HD
    queries = queries.astype(BF)
    stacked = jnp.concatenate([queries[:, h * HD : (h + 1) * HD] for h in range(heads)], axis=0)
    scores = dot_t(stacked, keys.astype(BF)) * HD ** (-0.5)
    mask = jnp.concatenate([mask_ref[...]] * heads, axis=0)
    scores = jnp.where(mask > 0.5, scores, -1e30)
    exponent = jnp.exp(scores - jnp.max(scores, axis=-1, keepdims=True))
    probs = (exponent / jnp.sum(exponent, axis=-1, keepdims=True)).astype(BF)
    context = dot(probs, values.astype(BF)).astype(BF)
    context = jnp.concatenate([context[h * rows : (h + 1) * rows] for h in range(heads)], axis=1)
    for b in range(blocks):
        waits[b][3].wait()
        out_ref[b] = dot(context, wo[b]).astype(BF)


def decoder_layer(which, blocks, gains, mask, own, other):
    count, rows, depth = blocks.shape
    q_cols, kv_cols = own[0].shape[1], own[1].shape[1]
    weights = count * depth * (2 * q_cols + 2 * kv_cols)
    return pl.pallas_call(
        layer_kernel,
        out_shape=jax.ShapeDtypeStruct(blocks.shape, BF),
        in_specs=[smem(), anywhere(), vmem(), vmem(), vmem()] + [anywhere()] * 8,
        out_specs=vmem(),
        scratch_shapes=[
            pltpu.VMEM(blocks.shape, BF),
            pltpu.VMEM((count, depth, q_cols), BF),
            pltpu.VMEM((count, depth, kv_cols), BF),
            pltpu.VMEM((count, depth, kv_cols), BF),
            pltpu.VMEM((count, q_cols, depth), BF),
            pltpu.SemaphoreType.DMA((5, count)),
        ],
        compiler_params=pltpu.CompilerParams(vmem_limit_bytes=60 << 20),
        cost_estimate=pl.CostEstimate(
            flops=2 * rows * weights, bytes_accessed=2 * weights, transcendentals=rows * rows * 4
        ),
        name="decoder_layer",
    )(which, blocks, *gains, mask, *own, *other)


def per_device(
    frames,
    ln_gain,
    ln_bias,
    enc_up,
    up_bias,
    enc_down,
    down_bias,
    adapt_in,
    adapt_out,
    lengths,
    routes,
    attn_gain,
    q_weight,
    k_weight,
    v_weight,
    o_weight,
):
    pool_count = lax.axis_size("pool")
    tp_count = lax.axis_size("tp")
    section_count = lax.axis_size("section")
    z_count = tp_count // 2
    pool_index = lax.axis_index("pool")
    section_index = lax.axis_index("section")
    tp_index = lax.axis_index("tp")
    z_index, y_low = tp_index // 2, tp_index % 2
    core, high = section_index % 2, section_index // 2
    z_groups = [[2 * z + y for z in range(z_count)] for y in range(2)]

    def chip_swap(value):
        return lax.ppermute(value, "section", [(i, i ^ 1) for i in range(section_count)])

    def y_move(value, moves):
        pairs = []
        for high_from, high_to, y_flip in moves:
            for c in range(2):
                for t in range(tp_count):
                    pairs.append(
                        (
                            (2 * high_from + c) * tp_count + t,
                            (2 * high_to + c) * tp_count + (t ^ y_flip),
                        )
                    )
        return lax.ppermute(value, ("section", "tp"), pairs)

    def z_all_to_all(value):
        return lax.all_to_all(
            value, "tp", split_axis=0, concat_axis=0, tiled=True, axis_index_groups=z_groups
        )

    def z_sum(partial):
        return jnp.sum(z_all_to_all(partial).astype(F32), axis=0)

    def z_move(value, step):
        pairs = []
        for section in range(section_count):
            turn_by = step if section % 2 == 0 else z_count - step
            for z in range(z_count):
                for y in range(2):
                    start = section * tp_count + y
                    pairs.append((start + 2 * z, start + 2 * ((z + turn_by) % z_count)))
        return lax.ppermute(value, ("section", "tp"), pairs)

    def z_scatter(parts):
        moved = [z_move(parts[step], step) for step in range(1, z_count)]
        return sum(part.astype(F32) for part in [parts[0]] + moved)

    def z_spread(shard):
        return [shard] + [z_move(shard, step) for step in range(1, z_count)]

    def z_gather(shard):
        return z_all_to_all(jnp.broadcast_to(shard[None], (z_count,) + shard.shape))

    def at_first(value):
        return jnp.where(y_low == 0, value, jnp.zeros_like(value))

    both = ((0, 0, 1), (1, 1, 1))

    own_layer = (q_weight[0], k_weight[0], v_weight[0], o_weight[0])
    early = [chip_swap(own_layer[0]), chip_swap(own_layer[3])]
    in_pair = (adapt_in.T, chip_swap(adapt_in.T))
    out_pair = (adapt_out, chip_swap(adapt_out))

    width = frames.shape[3]
    tokens = frames.shape[2] // STACK
    way = jnp.where(core == 0, 1, z_count - 1)
    place = jnp.stack([z_index, way]).astype(jnp.int32)
    partial_down = encoder(place, frames[0, 0], ln_gain, ln_bias, enc_up, up_bias, enc_down)
    own_frames = lax.dynamic_index_in_dim(
        frames[0, 0].reshape(tokens, STACK, width), z_index, 1, keepdims=False
    )
    extra = at_first(own_frames.astype(F32) + down_bias.astype(F32)[None])
    share = (z_scatter(partial_down) + extra).astype(BF)
    here = (share.astype(F32) + y_move(share, both).astype(F32)).astype(BF)
    here, in_pair, out_pair, early, own_layer = lax.optimization_barrier(
        (here, in_pair, out_pair, early, own_layer)
    )
    gains = [g.astype(F32).reshape(1, -1) for g in (attn_gain[0], chip_swap(attn_gain[0]))]
    other_layer = (early[0], chip_swap(own_layer[1]), chip_swap(own_layer[2]), early[1])
    there = y_move(here, ((0, 1, 1), (1, 0, 1)))
    encoded = jnp.where(high == 0, jnp.stack([here, there]), jnp.stack([there, here]))
    encoded = encoded.reshape(2 * tokens, width)

    share = z_scatter(adapter(place, z_spread(encoded), in_pair, out_pair)).astype(BF)
    summed = share.astype(F32) + y_move(share, both).astype(F32)
    from_high = y_move(summed.astype(BF), ((1, 0, 1),))
    hidden = (summed + from_high.astype(F32)).astype(BF)

    ends = jnp.cumsum(lengths[pool_index], axis=1, dtype=jnp.int32)
    token_ids = jnp.arange(tokens, dtype=jnp.int32)
    windows = jnp.sum(
        (ends[:, None, :] <= token_ids[None, :, None]).astype(jnp.int32), axis=2, dtype=jnp.int32
    )
    tags = windows + jnp.arange(section_count, dtype=jnp.int32)[:, None] * lengths.shape[2]
    tags = lax.dynamic_slice_in_dim(tags.reshape(2, 2, tokens), core, 1, 1).reshape(-1)
    row_ids = jnp.arange(2 * tokens, dtype=jnp.int32)
    allowed = (tags[:, None] == tags[None, :]) & (row_ids[None, :] <= row_ids[:, None])
    mask = allowed.astype(F32)

    tables = jax.vmap(
        jax.vmap(lambda route_row, length_row: slot_tables(route_row, length_row, pool_count, CAPW))
    )
    starts, spans = tables(routes[..., 0], lengths)
    offsets = jnp.arange(WIN_MAX, dtype=jnp.int32)

    def of_pair(table):
        pair = lax.dynamic_index_in_dim(table, pool_index, 0, keepdims=False)
        pair = pair.reshape((2, 2) + pair.shape[1:])
        pair = lax.dynamic_index_in_dim(pair, core, 1, keepdims=False)
        return jnp.transpose(pair, (0, 2, 1))

    row_valid = offsets < of_pair(spans)[..., None]
    row_index = of_pair(starts)[..., None] + offsets
    row_index = row_index + (jnp.arange(2, dtype=jnp.int32) * tokens)[:, None, None, None]
    row_index = jnp.where(row_valid, row_index, 0)

    for turn in range(4):
        which = (core != turn % 2).astype(jnp.int32)
        partial = decoder_layer(
            which.reshape(1), z_gather(hidden), gains, mask, own_layer, other_layer
        )
        share = (z_sum(partial) + at_first(hidden.astype(F32))).astype(BF)
        if turn == 1:
            moved = (y_move(share, ((0, 1, 0),)), y_move(share, ((0, 1, 1),)))
            hidden = sum(part.astype(F32) for part in moved).astype(BF)
        elif turn < 3:
            hidden = (share.astype(F32) + y_move(share, both).astype(F32)).astype(BF)

    picked = jnp.take(share, row_index.reshape(-1), axis=0)
    picked = jnp.where(row_valid.reshape(-1, 1), picked, jnp.zeros_like(picked))
    picked = picked.reshape(2, CAPW, pool_count, WIN_MAX, width)
    stay = lax.dynamic_index_in_dim(picked, y_low, 1, keepdims=False)
    leave = lax.dynamic_index_in_dim(picked, 1 - y_low, 1, keepdims=False)
    moved = (
        y_move(stay[0], ((1, 0, 0),)),
        y_move(leave[0], ((1, 0, 1),)),
        y_move(leave[1], ((1, 1, 1),)),
        jnp.where(high == 1, stay[1], jnp.zeros_like(stay[1])),
    )
    final = sum(part.astype(F32) for part in moved).astype(BF)
    landed = []
    for step in range(pool_count):
        pairs = []
        for x in range(pool_count):
            for z in range(z_count):
                for y in range(2):
                    pairs.append(
                        (
                            x * tp_count + 2 * z + y,
                            ((z + step) % pool_count) * tp_count + 2 * x + y,
                        )
                    )
        piece = lax.dynamic_index_in_dim(
            final, (z_index + step) % pool_count, 0, keepdims=False
        )
        landed.append(lax.ppermute(piece, ("pool", "tp"), pairs))
    landed = jnp.stack(landed)
    blocks = [
        lax.dynamic_index_in_dim(landed, (pool_index - z) % pool_count, 0, keepdims=False)
        for z in range(z_count)
    ]
    decoded = jnp.concatenate(blocks, axis=1).astype(F32)
    return decoded[None, None]


def solution(mesh):
    in_specs = (
        P("pool", "section", None, None),
        P(),
        P(),
        P(None, "tp"),
        P("tp"),
        P("tp", None),
        P(),
        P(None, ("section", "tp")),
        P(("section", "tp"), None),
        P(),
        P(),
        P("section", None),
        P("section", None, "tp"),
        P("section", None, "tp"),
        P("section", None, "tp"),
        P("section", "tp", None),
    )
    out_specs = P("pool", "section", "tp", None)
    return jax.shard_map(
        per_device, mesh=mesh, in_specs=in_specs, out_specs=out_specs, check_vma=False
    )
```

```python
import jax
import jax.numpy as jnp
from jax import lax
from jax.experimental import pallas as pl
from jax.experimental.pallas import tpu as pltpu
from jax.sharding import PartitionSpec as P

HD = 128
LANES = 128
WIN_MAX = 16
CAPW = 2
STACK = 4
EPSILON = 1e-05
BF = jnp.bfloat16
F32 = jnp.float32


def slot_tables(route_row, length_row, dest_count, capacity):
    windows = route_row.shape[0]
    window_ids = jnp.arange(windows, dtype=jnp.int32)
    starts = jnp.cumsum(length_row, dtype=jnp.int32) - length_row
    earlier = (route_row[None, :] == route_row[:, None]) & (
        window_ids[None, :] < window_ids[:, None]
    )
    window_rank = jnp.sum(earlier.astype(jnp.int32), axis=1, dtype=jnp.int32)
    dest_ids = jnp.arange(dest_count, dtype=jnp.int32)
    rank_ids = jnp.arange(capacity, dtype=jnp.int32)
    chosen = (route_row[None, None, :] == dest_ids[:, None, None]) & (
        window_rank[None, None, :] == rank_ids[None, :, None]
    )
    chosen = chosen.astype(jnp.int32)
    return (
        jnp.sum(chosen * starts, axis=2, dtype=jnp.int32),
        jnp.sum(chosen * length_row, axis=2, dtype=jnp.int32),
    )


def dot(a, b):
    return jnp.dot(a, b, preferred_element_type=F32)

def dot_t(a, b):
    return lax.dot_general(a, b, (((1,), (1,)), ((), ())), preferred_element_type=F32)


def exact_gelu(x):
    return 0.5 * x * (1.0 + lax.erf(x * (0.5**0.5)))


def vmem():
    return pl.BlockSpec(memory_space=pltpu.VMEM)


def anywhere():
    return pl.BlockSpec(memory_space=pl.ANY)


def smem():
    return pl.BlockSpec(memory_space=pltpu.SMEM)


def block_at(index, depth):
    return pl.ds(pl.multiple_of(index * depth, depth), depth)


def encoder_kernel(place, frames_ref, gain_ref, bias_ref, up_ref, up_bias_ref, down_ref, *rest):
    outs, (up_v, down_v, rows, sems) = rest[:STACK], rest[STACK:]
    copies = [
        pltpu.make_async_copy(up_ref, up_v, sems.at[0]),
        pltpu.make_async_copy(down_ref, down_v, sems.at[1]),
    ]
    for copy in copies:
        copy.start()
    values = frames_ref[...].astype(F32)
    centered = values - jnp.mean(values, axis=-1, keepdims=True)
    variance = jnp.mean(centered * centered, axis=-1, keepdims=True)
    normed = (
        centered * lax.rsqrt(variance + EPSILON) * gain_ref[...].astype(F32)[None]
        + bias_ref[...].astype(F32)[None]
    ).astype(BF)
    copies[0].wait()
    raised = dot(normed, up_v[...]) + up_bias_ref[...].astype(F32)[None]
    active = exact_gelu(raised).astype(BF)
    copies[1].wait()
    lowered = dot(active, down_v[...])
    count = outs[0].shape[0]
    for c in range(rows.shape[0]):
        cols = slice(c * LANES, (c + 1) * LANES)
        rows[c] = lowered[:, cols]
        for step in range(STACK):
            j = lax.rem(place[0] + place[1] * step, STACK)
            outs[step][:, cols] = rows[c, pl.ds(j, count, stride=STACK), :].astype(BF)


def encoder(place, frames, gain, bias, up, up_bias, down):
    count, width = frames.shape
    hidden = up.shape[1]
    return pl.pallas_call(
        encoder_kernel,
        out_shape=[jax.ShapeDtypeStruct((count // STACK, width), BF)] * STACK,
        in_specs=[smem(), vmem(), vmem(), vmem(), anywhere(), vmem(), anywhere()],
        out_specs=[vmem()] * STACK,
        scratch_shapes=[
            pltpu.VMEM((width, hidden), BF),
            pltpu.VMEM((hidden, width), BF),
            pltpu.VMEM((width // LANES, count, LANES), F32),
            pltpu.SemaphoreType.DMA((2,)),
        ],
        compiler_params=pltpu.CompilerParams(vmem_limit_bytes=56 << 20),
        cost_estimate=pl.CostEstimate(
            flops=4 * count * width * hidden,
            bytes_accessed=4 * width * hidden,
            transcendentals=count * hidden,
        ),
        name="encoder_units",
    )(place, frames, gain, bias, up, up_bias, down)


def adapter_kernel(place, x0, x1, x2, x3, in0, in1, out0, out1, *rest):
    xs, outs, (win, wout, sems) = (x0, x1, x2, x3), rest[:4], rest[4:]
    blocks, depth = len(xs), x0.shape[1]
    units = in0.shape[0]
    made = [[], []]
    for k in range(blocks):
        away = place[1] * k
        sources = (
            lax.rem(place[0] + blocks * blocks - away, blocks),
            lax.rem(place[0] + away, blocks),
        )
        for kind, pair in enumerate(((in0, in1), (out0, out1))):
            part = block_at(sources[kind], depth)
            for i in range(2):
                target = (win, wout)[kind].at[k, pl.ds(i * units, units), :]
                made[kind].append(
                    pltpu.make_async_copy(pair[i].at[:, part], target, sems.at[kind, i, k])
                )
    for copy in made[0] + made[1]:
        copy.start()
    total = 0.0
    for k in range(blocks):
        for copy in made[0][2 * k : 2 * k + 2]:
            copy.wait()
        total += dot_t(xs[k][...], win[k])
    lifted = exact_gelu(total).astype(BF)
    for k in range(blocks):
        for copy in made[1][2 * k : 2 * k + 2]:
            copy.wait()
        outs[k][...] = dot(lifted, wout[k]).astype(BF)


def adapter(place, blocks, in_pair, out_pair):
    units, width = in_pair[0].shape
    count, (rows, depth) = len(blocks), blocks[0].shape
    return pl.pallas_call(
        adapter_kernel,
        out_shape=[jax.ShapeDtypeStruct((rows, depth), BF)] * count,
        in_specs=[smem()] + [vmem()] * count + [anywhere()] * 4,
        out_specs=[vmem()] * count,
        scratch_shapes=[
            pltpu.VMEM((count, 2 * units, depth), BF),
            pltpu.VMEM((count, 2 * units, depth), BF),
            pltpu.SemaphoreType.DMA((2, 2, count)),
        ],
        compiler_params=pltpu.CompilerParams(vmem_limit_bytes=32 << 20),
        cost_estimate=pl.CostEstimate(
            flops=8 * rows * width * units,
            bytes_accessed=8 * width * units,
            transcendentals=2 * rows * units,
        ),
        name="adapter_units",
    )(place, *blocks, *in_pair, *out_pair)


def layer_kernel(
    which, x_hbm, gain0, gain1, mask_ref, q0, k0, v0, o0, q1, k1, v1, o1, out_ref, x_ref, wq, wk, wv, wo, sems
):
    blocks, rows, depth = x_ref.shape
    x_copies = [
        pltpu.make_async_copy(x_hbm.at[b], x_ref.at[b], sems.at[4, b]) for b in range(blocks)
    ]
    for copy in x_copies:
        copy.start()

    def copies(q_ref, k_ref, v_ref, o_ref):
        made = []
        for b in range(blocks):
            part = pl.ds(b * depth, depth)
            made.append(
                [
                    pltpu.make_async_copy(q_ref.at[part, :], wq.at[b], sems.at[0, b]),
                    pltpu.make_async_copy(k_ref.at[part, :], wk.at[b], sems.at[1, b]),
                    pltpu.make_async_copy(v_ref.at[part, :], wv.at[b], sems.at[2, b]),
                    pltpu.make_async_copy(o_ref.at[:, part], wo.at[b], sems.at[3, b]),
                ]
            )
        return made

    def begin(refs):
        made = copies(*refs)
        for group in made:
            for copy in group[:3]:
                copy.start()
        for group in made:
            group[3].start()

    @pl.when(which[0] == 0)
    def _():
        begin((q0, k0, v0, o0))

    @pl.when(which[0] != 0)
    def _():
        begin((q1, k1, v1, o1))

    waits = copies(q0, k0, v0, o0)
    for copy in x_copies:
        copy.wait()
    squares = sum(
        jnp.sum(jnp.square(x_ref[b].astype(F32)), axis=-1, keepdims=True) for b in range(blocks)
    )
    scale = lax.rsqrt(squares / (blocks * depth) + EPSILON)
    queries, keys, values = 0.0, 0.0, 0.0
    for b in range(blocks):
        cols = slice(b * depth, (b + 1) * depth)
        gain = jnp.where(which[0] == 0, gain0[:, cols], gain1[:, cols])
        normed = (x_ref[b].astype(F32) * scale * gain).astype(BF)
        for copy in waits[b][:3]:
            copy.wait()
        queries += dot(normed, wq[b])
        keys += dot(normed, wk[b])
        values += dot(normed, wv[b])
    heads = queries.shape[1] // HD
    queries = queries.astype(BF)
    stacked = jnp.concatenate([queries[:, h * HD : (h + 1) * HD] for h in range(heads)], axis=0)
    scores = dot_t(stacked, keys.astype(BF)) * HD ** (-0.5)
    mask = jnp.concatenate([mask_ref[...]] * heads, axis=0)
    scores = jnp.where(mask > 0.5, scores, -1e30)
    exponent = jnp.exp(scores - jnp.max(scores, axis=-1, keepdims=True))
    probs = (exponent / jnp.sum(exponent, axis=-1, keepdims=True)).astype(BF)
    context = dot(probs, values.astype(BF)).astype(BF)
    context = jnp.concatenate([context[h * rows : (h + 1) * rows] for h in range(heads)], axis=1)
    for b in range(blocks):
        waits[b][3].wait()
        out_ref[b] = dot(context, wo[b]).astype(BF)


def decoder_layer(which, blocks, gains, mask, own, other):
    count, rows, depth = blocks.shape
    q_cols, kv_cols = own[0].shape[1], own[1].shape[1]
    weights = count * depth * (2 * q_cols + 2 * kv_cols)
    return pl.pallas_call(
        layer_kernel,
        out_shape=jax.ShapeDtypeStruct(blocks.shape, BF),
        in_specs=[smem(), anywhere(), vmem(), vmem(), vmem()] + [anywhere()] * 8,
        out_specs=vmem(),
        scratch_shapes=[
            pltpu.VMEM(blocks.shape, BF),
            pltpu.VMEM((count, depth, q_cols), BF),
            pltpu.VMEM((count, depth, kv_cols), BF),
            pltpu.VMEM((count, depth, kv_cols), BF),
            pltpu.VMEM((count, q_cols, depth), BF),
            pltpu.SemaphoreType.DMA((5, count)),
        ],
        compiler_params=pltpu.CompilerParams(vmem_limit_bytes=50 << 20),
        cost_estimate=pl.CostEstimate(
            flops=2 * rows * weights, bytes_accessed=2 * weights, transcendentals=rows * rows * 4
        ),
        name="decoder_layer",
    )(which, blocks, *gains, mask, *own, *other)


def per_device(
    frames,
    ln_gain,
    ln_bias,
    enc_up,
    up_bias,
    enc_down,
    down_bias,
    adapt_in,
    adapt_out,
    lengths,
    routes,
    attn_gain,
    q_weight,
    k_weight,
    v_weight,
    o_weight,
):
    pool_count = lax.axis_size("pool")
    tp_count = lax.axis_size("tp")
    section_count = lax.axis_size("section")
    z_count = tp_count // 2
    pool_index = lax.axis_index("pool")
    section_index = lax.axis_index("section")
    tp_index = lax.axis_index("tp")
    z_index, y_low = tp_index // 2, tp_index % 2
    core, high = section_index % 2, section_index // 2
    z_groups = [[2 * z + y for z in range(z_count)] for y in range(2)]

    def chip_swap(value):
        return lax.ppermute(value, "section", [(i, i ^ 1) for i in range(section_count)])

    def y_move(value, moves):
        pairs = []
        for high_from, high_to, y_flip in moves:
            for c in range(2):
                for t in range(tp_count):
                    pairs.append(
                        (
                            (2 * high_from + c) * tp_count + t,
                            (2 * high_to + c) * tp_count + (t ^ y_flip),
                        )
                    )
        return lax.ppermute(value, ("section", "tp"), pairs)

    def z_all_to_all(value):
        return lax.all_to_all(
            value, "tp", split_axis=0, concat_axis=0, tiled=True, axis_index_groups=z_groups
        )

    def z_sum(partial):
        return jnp.sum(z_all_to_all(partial).astype(F32), axis=0)

    def z_move(value, step):
        pairs = []
        for section in range(section_count):
            turn_by = step if section % 2 == 0 else z_count - step
            for z in range(z_count):
                for y in range(2):
                    start = section * tp_count + y
                    pairs.append((start + 2 * z, start + 2 * ((z + turn_by) % z_count)))
        return lax.ppermute(value, ("section", "tp"), pairs)

    def z_scatter(parts):
        moved = [z_move(parts[step], step) for step in range(1, z_count)]
        return sum(part.astype(F32) for part in [parts[0]] + moved)

    def z_spread(shard):
        return [shard] + [z_move(shard, step) for step in range(1, z_count)]

    def z_gather(shard):
        return z_all_to_all(jnp.broadcast_to(shard[None], (z_count,) + shard.shape))

    def at_first(value):
        return jnp.where(y_low == 0, value, jnp.zeros_like(value))

    both = ((0, 0, 1), (1, 1, 1))

    own_layer = (q_weight[0], k_weight[0], v_weight[0], o_weight[0])
    early = [chip_swap(own_layer[0]), chip_swap(own_layer[3])]
    in_pair = (adapt_in.T, chip_swap(adapt_in.T))
    out_pair = (adapt_out, chip_swap(adapt_out))

    width = frames.shape[3]
    tokens = frames.shape[2] // STACK
    way = jnp.where(core == 0, 1, z_count - 1)
    place = jnp.stack([z_index, way]).astype(jnp.int32)
    partial_down = encoder(place, frames[0, 0], ln_gain, ln_bias, enc_up, up_bias, enc_down)
    own_frames = lax.dynamic_index_in_dim(
        frames[0, 0].reshape(tokens, STACK, width), z_index, 1, keepdims=False
    )
    extra = at_first(own_frames.astype(F32) + down_bias.astype(F32)[None])
    share = (z_scatter(partial_down) + extra).astype(BF)
    here = (share.astype(F32) + y_move(share, both).astype(F32)).astype(BF)
    here, in_pair, out_pair, early, own_layer = lax.optimization_barrier(
        (here, in_pair, out_pair, early, own_layer)
    )
    gains = [g.astype(F32).reshape(1, -1) for g in (attn_gain[0], chip_swap(attn_gain[0]))]
    other_layer = (early[0], chip_swap(own_layer[1]), chip_swap(own_layer[2]), early[1])
    there = y_move(here, ((0, 1, 1), (1, 0, 1)))
    encoded = jnp.where(high == 0, jnp.stack([here, there]), jnp.stack([there, here]))
    encoded = encoded.reshape(2 * tokens, width)

    share = z_scatter(adapter(place, z_spread(encoded), in_pair, out_pair)).astype(BF)
    summed = share.astype(F32) + y_move(share, both).astype(F32)
    from_high = y_move(summed.astype(BF), ((1, 0, 1),))
    hidden = (summed + from_high.astype(F32)).astype(BF)

    ends = jnp.cumsum(lengths[pool_index], axis=1, dtype=jnp.int32)
    token_ids = jnp.arange(tokens, dtype=jnp.int32)
    windows = jnp.sum(
        (ends[:, None, :] <= token_ids[None, :, None]).astype(jnp.int32), axis=2, dtype=jnp.int32
    )
    tags = windows + jnp.arange(section_count, dtype=jnp.int32)[:, None] * lengths.shape[2]
    tags = lax.dynamic_slice_in_dim(tags.reshape(2, 2, tokens), core, 1, 1).reshape(-1)
    row_ids = jnp.arange(2 * tokens, dtype=jnp.int32)
    allowed = (tags[:, None] == tags[None, :]) & (row_ids[None, :] <= row_ids[:, None])
    mask = allowed.astype(F32)

    tables = jax.vmap(
        jax.vmap(lambda route_row, length_row: slot_tables(route_row, length_row, pool_count, CAPW))
    )
    starts, spans = tables(routes[..., 0], lengths)
    offsets = jnp.arange(WIN_MAX, dtype=jnp.int32)

    def of_pair(table):
        pair = lax.dynamic_index_in_dim(table, pool_index, 0, keepdims=False)
        pair = pair.reshape((2, 2) + pair.shape[1:])
        pair = lax.dynamic_index_in_dim(pair, core, 1, keepdims=False)
        return jnp.transpose(pair, (0, 2, 1))

    row_valid = offsets < of_pair(spans)[..., None]
    row_index = of_pair(starts)[..., None] + offsets
    row_index = row_index + (jnp.arange(2, dtype=jnp.int32) * tokens)[:, None, None, None]
    row_index = jnp.where(row_valid, row_index, 0)

    for turn in range(4):
        which = (core != turn % 2).astype(jnp.int32)
        partial = decoder_layer(
            which.reshape(1), z_gather(hidden), gains, mask, own_layer, other_layer
        )
        share = (z_sum(partial) + at_first(hidden.astype(F32))).astype(BF)
        if turn == 1:
            moved = (y_move(share, ((0, 1, 0),)), y_move(share, ((0, 1, 1),)))
            hidden = sum(part.astype(F32) for part in moved).astype(BF)
        elif turn < 3:
            hidden = (share.astype(F32) + y_move(share, both).astype(F32)).astype(BF)

    picked = jnp.take(share, row_index.reshape(-1), axis=0)
    picked = jnp.where(row_valid.reshape(-1, 1), picked, jnp.zeros_like(picked))
    picked = picked.reshape(2, CAPW, pool_count, WIN_MAX, width)
    stay = lax.dynamic_index_in_dim(picked, y_low, 1, keepdims=False)
    leave = lax.dynamic_index_in_dim(picked, 1 - y_low, 1, keepdims=False)
    moved = (
        y_move(stay[0], ((1, 0, 0),)),
        y_move(leave[0], ((1, 0, 1),)),
        y_move(leave[1], ((1, 1, 1),)),
        jnp.where(high == 1, stay[1], jnp.zeros_like(stay[1])),
    )
    final = sum(part.astype(F32) for part in moved).astype(BF)
    landed = []
    for step in range(pool_count):
        pairs = []
        for x in range(pool_count):
            for z in range(z_count):
                for y in range(2):
                    pairs.append(
                        (
                            x * tp_count + 2 * z + y,
                            ((z + step) % pool_count) * tp_count + 2 * x + y,
                        )
                    )
        piece = lax.dynamic_index_in_dim(
            final, (z_index + step) % pool_count, 0, keepdims=False
        )
        landed.append(lax.ppermute(piece, ("pool", "tp"), pairs))
    landed = jnp.stack(landed)
    blocks = [
        lax.dynamic_index_in_dim(landed, (pool_index - z) % pool_count, 0, keepdims=False)
        for z in range(z_count)
    ]
    decoded = jnp.concatenate(blocks, axis=1).astype(F32)
    return decoded[None, None]


def solution(mesh):
    in_specs = (
        P("pool", "section", None, None),
        P(),
        P(),
        P(None, "tp"),
        P("tp"),
        P("tp", None),
        P(),
        P(None, ("section", "tp")),
        P(("section", "tp"), None),
        P(),
        P(),
        P("section", None),
        P("section", None, "tp"),
        P("section", None, "tp"),
        P("section", None, "tp"),
        P("section", "tp", None),
    )
    out_specs = P("pool", "section", "tp", None)
    return jax.shard_map(
        per_device, mesh=mesh, in_specs=in_specs, out_specs=out_specs, check_vma=False
    )
```

```python
import jax
import jax.numpy as jnp
from jax import lax
from jax.experimental import pallas as pl
from jax.experimental.pallas import tpu as pltpu
from jax.sharding import PartitionSpec as P

HD = 128
LANES = 128
WIN_MAX = 16
CAPW = 2
STACK = 4
EPSILON = 1e-05
BF = jnp.bfloat16
F32 = jnp.float32


def slot_tables(route_row, length_row, dest_count, capacity):
    windows = route_row.shape[0]
    window_ids = jnp.arange(windows, dtype=jnp.int32)
    starts = jnp.cumsum(length_row, dtype=jnp.int32) - length_row
    earlier = (route_row[None, :] == route_row[:, None]) & (
        window_ids[None, :] < window_ids[:, None]
    )
    window_rank = jnp.sum(earlier.astype(jnp.int32), axis=1, dtype=jnp.int32)
    dest_ids = jnp.arange(dest_count, dtype=jnp.int32)
    rank_ids = jnp.arange(capacity, dtype=jnp.int32)
    chosen = (route_row[None, None, :] == dest_ids[:, None, None]) & (
        window_rank[None, None, :] == rank_ids[None, :, None]
    )
    chosen = chosen.astype(jnp.int32)
    return (
        jnp.sum(chosen * starts, axis=2, dtype=jnp.int32),
        jnp.sum(chosen * length_row, axis=2, dtype=jnp.int32),
    )


def dot(a, b):
    return jnp.dot(a, b, preferred_element_type=F32)

def dot_t(a, b):
    return lax.dot_general(a, b, (((1,), (1,)), ((), ())), preferred_element_type=F32)


def exact_gelu(x):
    return 0.5 * x * (1.0 + lax.erf(x * (0.5**0.5)))


def vmem():
    return pl.BlockSpec(memory_space=pltpu.VMEM)


def anywhere():
    return pl.BlockSpec(memory_space=pl.ANY)


def smem():
    return pl.BlockSpec(memory_space=pltpu.SMEM)


def block_at(index, depth):
    return pl.ds(pl.multiple_of(index * depth, depth), depth)


def encoder_kernel(place, frames_ref, gain_ref, bias_ref, up_ref, up_bias_ref, down_ref, *rest):
    outs, (up_v, down_v, rows, sems) = rest[:STACK], rest[STACK:]
    copies = [
        pltpu.make_async_copy(up_ref, up_v, sems.at[0]),
        pltpu.make_async_copy(down_ref, down_v, sems.at[1]),
    ]
    for copy in copies:
        copy.start()
    values = frames_ref[...].astype(F32)
    centered = values - jnp.mean(values, axis=-1, keepdims=True)
    variance = jnp.mean(centered * centered, axis=-1, keepdims=True)
    normed = (
        centered * lax.rsqrt(variance + EPSILON) * gain_ref[...].astype(F32)[None]
        + bias_ref[...].astype(F32)[None]
    ).astype(BF)
    copies[0].wait()
    raised = dot(normed, up_v[...]) + up_bias_ref[...].astype(F32)[None]
    active = exact_gelu(raised).astype(BF)
    copies[1].wait()
    lowered = dot(active, down_v[...])
    count = outs[0].shape[0]
    for c in range(rows.shape[0]):
        cols = slice(c * LANES, (c + 1) * LANES)
        rows[c] = lowered[:, cols]
        for step in range(STACK):
            j = lax.rem(place[0] + place[1] * step, STACK)
            outs[step][:, cols] = rows[c, pl.ds(j, count, stride=STACK), :].astype(BF)


def encoder(place, frames, gain, bias, up, up_bias, down):
    count, width = frames.shape
    hidden = up.shape[1]
    return pl.pallas_call(
        encoder_kernel,
        out_shape=[jax.ShapeDtypeStruct((count // STACK, width), BF)] * STACK,
        in_specs=[smem(), vmem(), vmem(), vmem(), anywhere(), vmem(), anywhere()],
        out_specs=[vmem()] * STACK,
        scratch_shapes=[
            pltpu.VMEM((width, hidden), BF),
            pltpu.VMEM((hidden, width), BF),
            pltpu.VMEM((width // LANES, count, LANES), F32),
            pltpu.SemaphoreType.DMA((2,)),
        ],
        compiler_params=pltpu.CompilerParams(vmem_limit_bytes=56 << 20),
        cost_estimate=pl.CostEstimate(
            flops=4 * count * width * hidden,
            bytes_accessed=4 * width * hidden,
            transcendentals=count * hidden,
        ),
        name="encoder_units",
    )(place, frames, gain, bias, up, up_bias, down)


def adapter_kernel(place, x0, x1, x2, x3, in0, in1, out0, out1, *rest):
    xs, outs, (win, wout, sems) = (x0, x1, x2, x3), rest[:4], rest[4:]
    blocks, depth = len(xs), x0.shape[1]
    units = in0.shape[0]
    made = [[], []]
    for k in range(blocks):
        away = place[1] * k
        sources = (
            lax.rem(place[0] + blocks * blocks - away, blocks),
            lax.rem(place[0] + away, blocks),
        )
        for kind, pair in enumerate(((in0, in1), (out0, out1))):
            part = block_at(sources[kind], depth)
            for i in range(2):
                target = (win, wout)[kind].at[k, pl.ds(i * units, units), :]
                made[kind].append(
                    pltpu.make_async_copy(pair[i].at[:, part], target, sems.at[kind, i, k])
                )
    for copy in made[0] + made[1]:
        copy.start()
    total = 0.0
    for k in range(blocks):
        for copy in made[0][2 * k : 2 * k + 2]:
            copy.wait()
        total += dot_t(xs[k][...], win[k])
    lifted = exact_gelu(total).astype(BF)
    for k in range(blocks):
        for copy in made[1][2 * k : 2 * k + 2]:
            copy.wait()
        outs[k][...] = dot(lifted, wout[k]).astype(BF)


def adapter(place, blocks, in_pair, out_pair):
    units, width = in_pair[0].shape
    count, (rows, depth) = len(blocks), blocks[0].shape
    return pl.pallas_call(
        adapter_kernel,
        out_shape=[jax.ShapeDtypeStruct((rows, depth), BF)] * count,
        in_specs=[smem()] + [vmem()] * count + [anywhere()] * 4,
        out_specs=[vmem()] * count,
        scratch_shapes=[
            pltpu.VMEM((count, 2 * units, depth), BF),
            pltpu.VMEM((count, 2 * units, depth), BF),
            pltpu.SemaphoreType.DMA((2, 2, count)),
        ],
        compiler_params=pltpu.CompilerParams(vmem_limit_bytes=32 << 20),
        cost_estimate=pl.CostEstimate(
            flops=8 * rows * width * units,
            bytes_accessed=8 * width * units,
            transcendentals=2 * rows * units,
        ),
        name="adapter_units",
    )(place, *blocks, *in_pair, *out_pair)


def layer_kernel(
    which, x_hbm, gain0, gain1, mask_ref, q0, k0, v0, o0, q1, k1, v1, o1, out_ref, x_ref, wq, wk, wv, wo, sems
):
    blocks, rows, depth = x_ref.shape
    x_copies = [
        pltpu.make_async_copy(x_hbm.at[b], x_ref.at[b], sems.at[4, b]) for b in range(blocks)
    ]
    for copy in x_copies:
        copy.start()

    def copies(q_ref, k_ref, v_ref, o_ref):
        made = []
        for b in range(blocks):
            part = pl.ds(b * depth, depth)
            made.append(
                [
                    pltpu.make_async_copy(q_ref.at[part, :], wq.at[b], sems.at[0, b]),
                    pltpu.make_async_copy(k_ref.at[part, :], wk.at[b], sems.at[1, b]),
                    pltpu.make_async_copy(v_ref.at[part, :], wv.at[b], sems.at[2, b]),
                    pltpu.make_async_copy(o_ref.at[:, part], wo.at[b], sems.at[3, b]),
                ]
            )
        return made

    def begin(refs):
        made = copies(*refs)
        for group in made:
            for copy in group[:3]:
                copy.start()
        for group in made:
            group[3].start()

    @pl.when(which[0] == 0)
    def _():
        begin((q0, k0, v0, o0))

    @pl.when(which[0] != 0)
    def _():
        begin((q1, k1, v1, o1))

    waits = copies(q0, k0, v0, o0)
    for copy in x_copies:
        copy.wait()
    squares = sum(
        jnp.sum(jnp.square(x_ref[b].astype(F32)), axis=-1, keepdims=True) for b in range(blocks)
    )
    scale = lax.rsqrt(squares / (blocks * depth) + EPSILON)
    queries, keys, values = 0.0, 0.0, 0.0
    for b in range(blocks):
        cols = slice(b * depth, (b + 1) * depth)
        gain = jnp.where(which[0] == 0, gain0[:, cols], gain1[:, cols])
        normed = (x_ref[b].astype(F32) * scale * gain).astype(BF)
        for copy in waits[b][:3]:
            copy.wait()
        queries += dot(normed, wq[b])
        keys += dot(normed, wk[b])
        values += dot(normed, wv[b])
    heads = queries.shape[1] // HD
    queries = queries.astype(BF)
    stacked = jnp.concatenate([queries[:, h * HD : (h + 1) * HD] for h in range(heads)], axis=0)
    scores = dot_t(stacked, keys.astype(BF)) * HD ** (-0.5)
    mask = jnp.concatenate([mask_ref[...]] * heads, axis=0)
    scores = jnp.where(mask > 0.5, scores, -1e30)
    exponent = jnp.exp(scores - jnp.max(scores, axis=-1, keepdims=True))
    probs = (exponent / jnp.sum(exponent, axis=-1, keepdims=True)).astype(BF)
    context = dot(probs, values.astype(BF)).astype(BF)
    context = jnp.concatenate([context[h * rows : (h + 1) * rows] for h in range(heads)], axis=1)
    for b in range(blocks):
        waits[b][3].wait()
        out_ref[b] = dot(context, wo[b]).astype(BF)


def decoder_layer(which, blocks, gains, mask, own, other):
    count, rows, depth = blocks.shape
    q_cols, kv_cols = own[0].shape[1], own[1].shape[1]
    weights = count * depth * (2 * q_cols + 2 * kv_cols)
    return pl.pallas_call(
        layer_kernel,
        out_shape=jax.ShapeDtypeStruct(blocks.shape, BF),
        in_specs=[smem(), anywhere(), vmem(), vmem(), vmem()] + [anywhere()] * 8,
        out_specs=vmem(),
        scratch_shapes=[
            pltpu.VMEM(blocks.shape, BF),
            pltpu.VMEM((count, depth, q_cols), BF),
            pltpu.VMEM((count, depth, kv_cols), BF),
            pltpu.VMEM((count, depth, kv_cols), BF),
            pltpu.VMEM((count, q_cols, depth), BF),
            pltpu.SemaphoreType.DMA((5, count)),
        ],
        compiler_params=pltpu.CompilerParams(vmem_limit_bytes=47 << 20),
        cost_estimate=pl.CostEstimate(
            flops=2 * rows * weights, bytes_accessed=2 * weights, transcendentals=rows * rows * 4
        ),
        name="decoder_layer",
    )(which, blocks, *gains, mask, *own, *other)


def per_device(
    frames,
    ln_gain,
    ln_bias,
    enc_up,
    up_bias,
    enc_down,
    down_bias,
    adapt_in,
    adapt_out,
    lengths,
    routes,
    attn_gain,
    q_weight,
    k_weight,
    v_weight,
    o_weight,
):
    pool_count = lax.axis_size("pool")
    tp_count = lax.axis_size("tp")
    section_count = lax.axis_size("section")
    z_count = tp_count // 2
    pool_index = lax.axis_index("pool")
    section_index = lax.axis_index("section")
    tp_index = lax.axis_index("tp")
    z_index, y_low = tp_index // 2, tp_index % 2
    core, high = section_index % 2, section_index // 2
    z_groups = [[2 * z + y for z in range(z_count)] for y in range(2)]

    def chip_swap(value):
        return lax.ppermute(value, "section", [(i, i ^ 1) for i in range(section_count)])

    def y_move(value, moves):
        pairs = []
        for high_from, high_to, y_flip in moves:
            for c in range(2):
                for t in range(tp_count):
                    pairs.append(
                        (
                            (2 * high_from + c) * tp_count + t,
                            (2 * high_to + c) * tp_count + (t ^ y_flip),
                        )
                    )
        return lax.ppermute(value, ("section", "tp"), pairs)

    def z_all_to_all(value):
        return lax.all_to_all(
            value, "tp", split_axis=0, concat_axis=0, tiled=True, axis_index_groups=z_groups
        )

    def z_sum(partial):
        return jnp.sum(z_all_to_all(partial).astype(F32), axis=0)

    def z_move(value, step):
        pairs = []
        for section in range(section_count):
            turn_by = step if section % 2 == 0 else z_count - step
            for z in range(z_count):
                for y in range(2):
                    start = section * tp_count + y
                    pairs.append((start + 2 * z, start + 2 * ((z + turn_by) % z_count)))
        return lax.ppermute(value, ("section", "tp"), pairs)

    def z_scatter(parts):
        moved = [z_move(parts[step], step) for step in range(1, z_count)]
        return sum(part.astype(F32) for part in [parts[0]] + moved)

    def z_spread(shard):
        return [shard] + [z_move(shard, step) for step in range(1, z_count)]

    def z_gather(shard):
        return z_all_to_all(jnp.broadcast_to(shard[None], (z_count,) + shard.shape))

    def at_first(value):
        return jnp.where(y_low == 0, value, jnp.zeros_like(value))

    both = ((0, 0, 1), (1, 1, 1))

    own_layer = (q_weight[0], k_weight[0], v_weight[0], o_weight[0])
    early = [chip_swap(own_layer[0]), chip_swap(own_layer[3])]
    in_pair = (adapt_in.T, chip_swap(adapt_in.T))
    out_pair = (adapt_out, chip_swap(adapt_out))

    width = frames.shape[3]
    tokens = frames.shape[2] // STACK
    way = jnp.where(core == 0, 1, z_count - 1)
    place = jnp.stack([z_index, way]).astype(jnp.int32)
    partial_down = encoder(place, frames[0, 0], ln_gain, ln_bias, enc_up, up_bias, enc_down)
    own_frames = lax.dynamic_index_in_dim(
        frames[0, 0].reshape(tokens, STACK, width), z_index, 1, keepdims=False
    )
    extra = at_first(own_frames.astype(F32) + down_bias.astype(F32)[None])
    share = (z_scatter(partial_down) + extra).astype(BF)
    here = (share.astype(F32) + y_move(share, both).astype(F32)).astype(BF)
    here, in_pair, out_pair, early, own_layer = lax.optimization_barrier(
        (here, in_pair, out_pair, early, own_layer)
    )
    gains = [g.astype(F32).reshape(1, -1) for g in (attn_gain[0], chip_swap(attn_gain[0]))]
    other_layer = (early[0], chip_swap(own_layer[1]), chip_swap(own_layer[2]), early[1])
    there = y_move(here, ((0, 1, 1), (1, 0, 1)))
    encoded = jnp.where(high == 0, jnp.stack([here, there]), jnp.stack([there, here]))
    encoded = encoded.reshape(2 * tokens, width)

    share = z_scatter(adapter(place, z_spread(encoded), in_pair, out_pair)).astype(BF)
    summed = share.astype(F32) + y_move(share, both).astype(F32)
    from_high = y_move(summed.astype(BF), ((1, 0, 1),))
    hidden = (summed + from_high.astype(F32)).astype(BF)

    ends = jnp.cumsum(lengths[pool_index], axis=1, dtype=jnp.int32)
    token_ids = jnp.arange(tokens, dtype=jnp.int32)
    windows = jnp.sum(
        (ends[:, None, :] <= token_ids[None, :, None]).astype(jnp.int32), axis=2, dtype=jnp.int32
    )
    tags = windows + jnp.arange(section_count, dtype=jnp.int32)[:, None] * lengths.shape[2]
    tags = lax.dynamic_slice_in_dim(tags.reshape(2, 2, tokens), core, 1, 1).reshape(-1)
    row_ids = jnp.arange(2 * tokens, dtype=jnp.int32)
    allowed = (tags[:, None] == tags[None, :]) & (row_ids[None, :] <= row_ids[:, None])
    mask = allowed.astype(F32)

    tables = jax.vmap(
        jax.vmap(lambda route_row, length_row: slot_tables(route_row, length_row, pool_count, CAPW))
    )
    starts, spans = tables(routes[..., 0], lengths)
    offsets = jnp.arange(WIN_MAX, dtype=jnp.int32)

    def of_pair(table):
        pair = lax.dynamic_index_in_dim(table, pool_index, 0, keepdims=False)
        pair = pair.reshape((2, 2) + pair.shape[1:])
        pair = lax.dynamic_index_in_dim(pair, core, 1, keepdims=False)
        return jnp.transpose(pair, (0, 2, 1))

    row_valid = offsets < of_pair(spans)[..., None]
    row_index = of_pair(starts)[..., None] + offsets
    row_index = row_index + (jnp.arange(2, dtype=jnp.int32) * tokens)[:, None, None, None]
    row_index = jnp.where(row_valid, row_index, 0)

    for turn in range(4):
        which = (core != turn % 2).astype(jnp.int32)
        partial = decoder_layer(
            which.reshape(1), z_gather(hidden), gains, mask, own_layer, other_layer
        )
        share = (z_sum(partial) + at_first(hidden.astype(F32))).astype(BF)
        if turn == 1:
            moved = (y_move(share, ((0, 1, 0),)), y_move(share, ((0, 1, 1),)))
            hidden = sum(part.astype(F32) for part in moved).astype(BF)
        elif turn < 3:
            hidden = (share.astype(F32) + y_move(share, both).astype(F32)).astype(BF)

    picked = jnp.take(share, row_index.reshape(-1), axis=0)
    picked = jnp.where(row_valid.reshape(-1, 1), picked, jnp.zeros_like(picked))
    picked = picked.reshape(2, CAPW, pool_count, WIN_MAX, width)
    stay = lax.dynamic_index_in_dim(picked, y_low, 1, keepdims=False)
    leave = lax.dynamic_index_in_dim(picked, 1 - y_low, 1, keepdims=False)
    moved = (
        y_move(stay[0], ((1, 0, 0),)),
        y_move(leave[0], ((1, 0, 1),)),
        y_move(leave[1], ((1, 1, 1),)),
        jnp.where(high == 1, stay[1], jnp.zeros_like(stay[1])),
    )
    final = sum(part.astype(F32) for part in moved).astype(BF)
    landed = []
    for step in range(pool_count):
        pairs = []
        for x in range(pool_count):
            for z in range(z_count):
                for y in range(2):
                    pairs.append(
                        (
                            x * tp_count + 2 * z + y,
                            ((z + step) % pool_count) * tp_count + 2 * x + y,
                        )
                    )
        piece = lax.dynamic_index_in_dim(
            final, (z_index + step) % pool_count, 0, keepdims=False
        )
        landed.append(lax.ppermute(piece, ("pool", "tp"), pairs))
    landed = jnp.stack(landed)
    blocks = [
        lax.dynamic_index_in_dim(landed, (pool_index - z) % pool_count, 0, keepdims=False)
        for z in range(z_count)
    ]
    decoded = jnp.concatenate(blocks, axis=1).astype(F32)
    return decoded[None, None]


def solution(mesh):
    in_specs = (
        P("pool", "section", None, None),
        P(),
        P(),
        P(None, "tp"),
        P("tp"),
        P("tp", None),
        P(),
        P(None, ("section", "tp")),
        P(("section", "tp"), None),
        P(),
        P(),
        P("section", None),
        P("section", None, "tp"),
        P("section", None, "tp"),
        P("section", None, "tp"),
        P("section", "tp", None),
    )
    out_specs = P("pool", "section", "tp", None)
    return jax.shard_map(
        per_device, mesh=mesh, in_specs=in_specs, out_specs=out_specs, check_vma=False
    )
```
